512 devices in a mesh: serve: 64 (over y, z), head: 8 (over x, core).
Axes of the slice: x: 4, y: 8, z: 8, core: 2. Of those that a mesh axis runs over, the one named last changes fastest.
Arguments:
- pre_x: bfloat16 [16384, 4096], P(('serve', 'head')), may hold values from -6 to 6
- pre_z: bfloat16 [16384, 4096], P(('serve', 'head')), may hold values from -6 to 6
- pre_b: bfloat16 [16384, 1024], P(('serve', 'head')), may hold values from -0.59765625 to 0.59765625
- pre_c: bfloat16 [16384, 1024], P(('serve', 'head')), may hold values from -0.59765625 to 0.59765625
- pre_dt: bfloat16 [16384, 64], P(('serve', 'head')), may hold values from -3 to 3
- suffix_lengths: int32 [64, 3], P('serve'), may hold values from 1 to 128, 256 in all within a row
- prefix_hits: int32 [192], replicated, may hold values from 0 to 255
- snapshot_slots: int32 [192], replicated, may hold values from 0 to 255, as said below
- cache_states: float32 [256, 64, 64, 128], P('serve', 'head'), may hold values from -6 to 6
- dec_x: bfloat16 [128, 4096], P('serve', 'head'), may hold values from -6 to 6
- dec_z: bfloat16 [128, 4096], P('serve', 'head'), may hold values from -6 to 6
- dec_b: bfloat16 [128, 1024], P('serve', 'head'), may hold values from -0.59765625 to 0.59765625
- dec_c: bfloat16 [128, 1024], P('serve', 'head'), may hold values from -0.59765625 to 0.59765625
- dec_dt: bfloat16 [128, 64], P('serve', 'head'), may hold values from -3 to 3
- dec_states: float32 [128, 64, 64, 128], P('serve', 'head'), may hold values from -6 to 6
- decay_rate: float32 [64], P('head'), may hold values from 0.001 to 0.04
- d_skip: float32 [64], P('head'), may hold values from 0.5 to 2
- norm_weight: float32 [4096], P('head'), may hold values from 0.5 to 1.5
Outputs:
- pre_out: bfloat16 [16384, 4096], P('serve', 'head')
- cache_out: float32 [256, 64, 64, 128], P('serve', 'head')
- dec_out: bfloat16 [128, 4096], P('serve', 'head')
- dec_new: float32 [128, 64, 64, 128], P('serve', 'head')
The draws below stay inside these ranges and needn't reach their ends.
Inputs may be any that keep to these rules, and one draw needn't show every extreme that they name: `snapshot_slots`: entries are distinct; each holder's block of 4 slots is named by exactly 3 entries. `prefix_hits`: entry r belongs to the (r mod 3)-th suffix of serving device r // 3.
All inputs are finite; a program needn't handle non-finite values.
Results may differ from the reference program's by a relative error of at most 0.0055.
Values may be sent and summed in bfloat16 or wider, within the bound.
No kernel may reach another device: no remote copies, remote signals or barrier semaphores. Data moves between devices by JAX's collectives and lax.ppermute only.
A program may use at most 64 MiB of HBM per device.

```python
import math
import jax
import jax.numpy as jnp
import numpy as np
from jax import lax

HEADS = 64
HEAD_DIM = 64
STATE = 128
GROUPS = 8
PACK = 256
PRE_DEV = 3
CACHE_DEV = 4
DIN = 4096
MOSTLEN = 128
TOKENS = 16384
PREFILLS = 192
SLOTS = 256
DECODES = 128
N_SERVE = 64


def draw_snapshot_slots(key, part):
    key = jax.random.fold_in(key, 7)
    holders = SLOTS // CACHE_DEV
    holder_keys = jax.random.split(key, holders + 1)
    shuffled = jax.vmap(lambda one_key: jax.random.permutation(one_key, CACHE_DEV))(holder_keys[1:]).astype(jnp.int32)
    holder_ids = jnp.arange(holders, dtype=jnp.int32)
    target = jnp.where(holder_ids == 0, 0, jnp.where(holder_ids == holders - 1, CACHE_DEV - 1, shuffled[:, 0])).astype(jnp.int32)
    rotated = (shuffled - shuffled[:, :1] + target[:, None] + CACHE_DEV) % CACHE_DEV
    chosen = rotated[:, :PRE_DEV]
    flat_slots = (holder_ids[:, None] * CACHE_DEV + chosen).reshape(-1)
    order = jax.random.permutation(holder_keys[0], flat_slots.shape[0])
    return flat_slots[order].astype(jnp.int32)


def set_ends(array, rng, least, high):
    longest = array.shape.index(max(array.shape))
    spots = []
    for shift in (0, 1):
        where = [jax.random.randint(jax.random.fold_in(rng, axis), (), 0, length) for axis, length in enumerate(array.shape)]
        where[longest] = (where[longest] + shift) % array.shape[longest]
        spots.append(tuple(where))
    return array.at[spots[0]].set(least).at[spots[1]].set(high)


def block_levels(rng, dims, shards, low, high):
    def one(dim, parts):
        draws = jax.random.uniform(jax.random.fold_in(jax.random.fold_in(rng, 6), dim), (parts,), jnp.float32, low / len(shards), high / len(shards))
        return jnp.repeat(jnp.exp(draws), dims[dim] // parts).reshape((-1,) + (1,) * (len(dims) - dim - 1))

    level = one(*shards[0])
    for cut in shards[1:]:
        level = level * one(*cut)
    return level


def rank_bounds(number_of, skew):
    loads = [(1 << 20) // math.isqrt(rank ** skew) + 1 for rank in range(1, number_of + 1)]
    width = 1 + sum(loads) // (1 << 30)
    return np.cumsum(np.array([max(1, weight // width) for weight in loads]))


def ranked(own_key, dims, number_of, lean):
    listing = rank_bounds(number_of, lean)
    ticket = jax.random.randint(jax.random.fold_in(own_key, 1), dims, 0, int(listing[number_of - 1]))
    standing = jnp.searchsorted(jnp.asarray(listing, jnp.int32), ticket, side="right")
    return jax.random.permutation(jax.random.fold_in(own_key, 2), number_of)[standing].astype(jnp.int32)


def profile(count, total, reach, slope):
    loads = [(1 << 20) // math.isqrt(rank ** slope) + 1 for rank in range(2, count + 1)]
    spare, holding = total - reach - (count - 1), [1] * (count - 1)
    while spare > 0:
        movable = [i for i in range(count - 1) if holding[i] < reach]
        whole, budget = sum([loads[i] for i in movable]), spare
        for i in movable:
            more = min(reach - holding[i], max(1, budget * loads[i] // whole), spare)
            holding[i] = holding[i] + more
            spare = spare - more
    return np.array([reach] + holding)


def uneven_parts(stream_key, amount, total, bound, slope):
    if amount == 2:
        one = jax.random.randint(stream_key, (), max(1, total - bound), min(bound, total - 1) + 1)
        return jnp.stack([one, total - one])
    tallies = jnp.asarray(profile(amount, total, bound, slope), jnp.int32)
    pairs = (amount - 1) // 2
    donor, receiver = tallies[1:1 + 2 * pairs:2], tallies[2:2 + 2 * pairs:2]
    room = jnp.minimum(donor - 1, bound - receiver)
    passed = jax.random.randint(jax.random.fold_in(stream_key, 1), (pairs,), 0, 1 << 20) % (room + 1)
    tallies = tallies.at[1:1 + 2 * pairs:2].set(donor - passed).at[2:2 + 2 * pairs:2].set(receiver + passed)
    return tallies[jax.random.permutation(jax.random.fold_in(stream_key, 2), amount)]


def noise(own_key, shape, scale, most, cuts=(), kind=jnp.bfloat16):
    gain = block_levels(own_key, shape, cuts, -0.22, 0.18) if cuts else 1.0
    array = jax.random.normal(own_key, shape, jnp.float32) * scale * gain
    return jnp.minimum(jnp.maximum(array, -most), most).astype(kind)


def setup_inputs(seed: int = 0) -> dict:
    streams_of = jax.random.split(jax.random.key(seed), 19)
    return {
        "pre_x": noise(streams_of[0], (TOKENS, DIN), 1.0, 6.0, ((0, 512),)),
        "pre_z": noise(streams_of[1], (TOKENS, DIN), 1.0, 6.0, ((0, 512),)),
        "pre_b": noise(streams_of[2], (TOKENS, GROUPS * STATE), (STATE ** -0.5), 0.59765625, ((0, 512),)),
        "pre_c": noise(streams_of[3], (TOKENS, GROUPS * STATE), (STATE ** -0.5), 0.59765625, ((0, 512),)),
        "pre_dt": noise(streams_of[4], (TOKENS, HEADS), 0.5, 3.0, ((0, 512),)),
        "suffix_lengths": jax.vmap(lambda own: uneven_parts(own, PRE_DEV, PACK, MOSTLEN, 1))(jax.random.split(streams_of[5], N_SERVE)).reshape((N_SERVE, PRE_DEV)).astype(jnp.int32),
        "prefix_hits": set_ends(ranked(streams_of[6], (PREFILLS,), SLOTS, 2), jax.random.fold_in(streams_of[6], 3), 0, SLOTS - 1).astype(jnp.int32),
        "snapshot_slots": draw_snapshot_slots(jax.random.fold_in(streams_of[18], 71), 0),
        "cache_states": noise(streams_of[8], (SLOTS, HEADS, HEAD_DIM, STATE), 1.0, 6.0, ((0, 64), (1, 8)), jnp.float32),
        "dec_x": noise(streams_of[9], (DECODES, DIN), 1.0, 6.0, ((0, 64), (1, 8))),
        "dec_z": noise(streams_of[10], (DECODES, DIN), 1.0, 6.0, ((0, 64), (1, 8))),
        "dec_b": noise(streams_of[11], (DECODES, GROUPS * STATE), (STATE ** -0.5), 0.59765625, ((0, 64), (1, 8))),
        "dec_c": noise(streams_of[12], (DECODES, GROUPS * STATE), (STATE ** -0.5), 0.59765625, ((0, 64), (1, 8))),
        "dec_dt": noise(streams_of[13], (DECODES, HEADS), 0.5, 3.0, ((0, 64), (1, 8))),
        "dec_states": noise(streams_of[14], (DECODES, HEADS, HEAD_DIM, STATE), 1.0, 6.0, ((0, 64), (1, 8)), jnp.float32),
        "decay_rate": jnp.clip(jnp.exp(math.log(0.04) - 3.6888794 * jax.random.uniform(streams_of[15], (HEADS,), jnp.float32) ** block_levels(streams_of[15], (HEADS,), ((0, 8),), -0.2, 0.2)), 0.001, 0.04),
        "d_skip": jnp.clip(0.5 + 1.5 * jax.random.uniform(streams_of[16], (HEADS,), jnp.float32) ** block_levels(streams_of[16], (HEADS,), ((0, 8),), -0.2, 0.2), 0.5, 2.0),
        "norm_weight": jnp.clip(1.0 + 0.1 * jax.random.normal(streams_of[17], (DIN,), jnp.float32), 0.5, 1.5),
    }


highest = lax.Precision.HIGHEST

def gated_norm(values, gate_in, norm_weight):
    shaped = values.shape
    gated = values * jax.nn.silu(gate_in.astype(jnp.float32).reshape(shaped))
    square_mean = lax.optimization_barrier(jnp.mean(gated * gated, axis=(2, 3), keepdims=True))
    normed = gated * lax.rsqrt(square_mean + 1e-05) * norm_weight.reshape(shaped[1:])
    return normed.reshape(shaped[0], -1).astype(jnp.bfloat16)

def segment_block(inputs, gate_in, b_proj, c_proj, step_raw, lengths, initial, head_rates, skip_gain, norm_weight):
    length = inputs.shape[0]
    head_count = step_raw.shape[1]
    groups = b_proj.shape[1] // STATE
    per_group = head_count // groups
    seg_ends = jnp.cumsum(lengths).astype(jnp.int32)
    starts = (seg_ends - lengths).astype(jnp.int32)
    position = jnp.arange(length, dtype=jnp.int32)
    seg_index = lax.optimization_barrier(jnp.sum((position[:, None] >= seg_ends[None, :]).astype(jnp.int32), axis=1))
    member = (seg_index[:, None] == jnp.arange(lengths.shape[0], dtype=jnp.int32)[None, :]).astype(jnp.float32)
    step_size = jax.nn.softplus(step_raw.astype(jnp.float32))
    log_decay = -step_size * head_rates[None, :]
    running = jnp.cumsum(log_decay, axis=0)
    before = running - log_decay
    seg_base = jnp.take(before, starts, axis=0)
    seg_end = jnp.take(running, seg_ends - 1, axis=0)
    tok_base = jnp.take(seg_base, seg_index, axis=0)
    tok_end = jnp.take(seg_end, seg_index, axis=0)
    allowed = (seg_index[:, None] == seg_index[None, :]) & (position[:, None] >= position[None, :])
    running_t = running.T
    decay_mat = jnp.exp(jnp.where(allowed[None], running_t[:, :, None] - running_t[:, None, :], -jnp.inf))
    b_group = b_proj.astype(jnp.float32).reshape(length, groups, STATE)
    c_group = c_proj.astype(jnp.float32).reshape(length, groups, STATE)
    scores = jnp.einsum('tgn,sgn->gts', c_group, b_group, precision=highest)
    weights = decay_mat.reshape(groups, per_group, length, length) * scores[:, None] * step_size.T.reshape(groups, per_group, 1, length)
    values = inputs.astype(jnp.float32).reshape(length, groups, per_group, HEAD_DIM)
    inner_out = jnp.einsum('gkts,sgkp->tgkp', weights, values, precision=highest)
    start_states = initial.reshape(-1, groups, per_group, HEAD_DIM, STATE)
    readout = jnp.einsum('tgn,jgkpn->tjgkp', c_group, start_states, precision=highest)
    carried = jnp.einsum('tj,tjgkp->tgkp', member, readout, precision=highest)
    carried = carried * jnp.exp(running - tok_base).reshape(length, groups, per_group, 1)
    outputs = inner_out + carried + skip_gain.reshape(groups, per_group, 1) * values
    result = gated_norm(outputs, gate_in, norm_weight)
    to_end = (jnp.exp(tok_end - running) * step_size).reshape(length, groups, per_group, 1) * values
    spread = member[:, :, None, None, None] * to_end[:, None]
    local_state = jnp.einsum('tjgkp,tgn->jgkpn', spread, b_group, precision=highest)
    kept_part = jnp.exp(seg_end - seg_base).reshape(-1, groups, per_group, 1, 1) * start_states
    finals = (kept_part + local_state).reshape(-1, head_count, HEAD_DIM, STATE)
    return (result, finals)

def decode_block(inputs, gate_in, b_proj, c_proj, step_raw, states, head_rates, skip_gain, norm_weight):
    row_count = inputs.shape[0]
    head_count = step_raw.shape[1]
    groups = b_proj.shape[1] // STATE
    per_group = head_count // groups
    step_size = jax.nn.softplus(step_raw.astype(jnp.float32))
    factor = jnp.exp(-step_size * head_rates[None, :]).reshape(row_count, groups, per_group, 1, 1)
    values = inputs.astype(jnp.float32).reshape(row_count, groups, per_group, HEAD_DIM)
    b_group = b_proj.astype(jnp.float32).reshape(row_count, groups, STATE)
    c_group = c_proj.astype(jnp.float32).reshape(row_count, groups, STATE)
    written = (step_size.reshape(row_count, groups, per_group, 1) * values)[..., None] * b_group[:, :, None, None, :]
    updated = factor * states.reshape(row_count, groups, per_group, HEAD_DIM, STATE) + written
    outputs = jnp.einsum('rgkpn,rgn->rgkp', updated, c_group, precision=highest) + skip_gain.reshape(groups, per_group, 1) * values
    return (gated_norm(outputs, gate_in, norm_weight), updated.reshape(row_count, head_count, HEAD_DIM, STATE))

def reference(pre_x, pre_z, pre_b, pre_c, pre_dt, suffix_lengths, prefix_hits, snapshot_slots, cache_states, dec_x, dec_z, dec_b, dec_c, dec_dt, dec_states, decay_rate, d_skip, norm_weight):
    pack_count = suffix_lengths.shape[0]

    def one_pack(pack_index):
        start_row = pack_index * PACK
        pieces = [lax.dynamic_slice_in_dim(source, start_row, PACK, 0) for source in (pre_x, pre_z, pre_b, pre_c, pre_dt)]
        hit_slots = lax.dynamic_slice_in_dim(prefix_hits, pack_index * PRE_DEV, PRE_DEV, 0)
        initial = jnp.take(cache_states, hit_slots, axis=0)
        lengths = lax.dynamic_index_in_dim(suffix_lengths, pack_index, 0, keepdims=False)
        return segment_block(pieces[0], pieces[1], pieces[2], pieces[3], pieces[4], lengths, initial, decay_rate, d_skip, norm_weight)
    results, finals = lax.map(one_pack, jnp.arange(pack_count, dtype=jnp.int32))
    pre_out = results.reshape(-1, results.shape[-1])
    cache_out = cache_states.at[snapshot_slots].set(finals.reshape((-1,) + cache_states.shape[1:]))
    dec_out, dec_new = decode_block(dec_x, dec_z, dec_b, dec_c, dec_dt, dec_states, decay_rate, d_skip, norm_weight)
    return (pre_out, cache_out, dec_out, dec_new)
```

```python
import jax
import jax.numpy as jnp
from jax import lax
from jax.experimental import pallas as pl
from jax.experimental.pallas import tpu as pltpu
from jax.sharding import PartitionSpec as P

HEAD_DIM = 64
STATE = 128
REQS = 3
SLOTS = 4
ROWS = 8

f32 = jnp.float32
bf16 = jnp.bfloat16
highest = lax.Precision.HIGHEST

ANY = pl.BlockSpec(memory_space=pl.ANY)
HBM = pl.BlockSpec(memory_space=pltpu.HBM)
VMEM = pl.BlockSpec(memory_space=pltpu.VMEM)
SMEM = pl.BlockSpec(memory_space=pltpu.SMEM)


def params(mib=12):
    return pltpu.CompilerParams(vmem_limit_bytes=mib * 1024 * 1024)


def cost(flops, moved):
    return pl.CostEstimate(flops=flops, bytes_accessed=moved, transcendentals=0)


def dot(a, b):
    return jnp.dot(a, b, preferred_element_type=f32)


def dot_nt(a, b):
    return lax.dot_general(a, b, (((1,), (1,)), ((), ())), preferred_element_type=f32)


def dot_tn(a, b):
    return lax.dot_general(a, b, (((0,), (0,)), ((), ())), preferred_element_type=f32)


def split(value, parts):
    pieces = []
    for _ in range(parts):
        piece = value.astype(bf16)
        pieces.append(piece)
        value = value - piece.astype(f32)
    return pieces


def exact_left(mask, value, parts=3):
    total = None
    for piece in split(value, parts):
        term = dot(mask, piece)
        total = term if total is None else total + term
    return total


def exact_right(value, mask, parts=3):
    total = None
    for piece in split(value, parts):
        term = dot(piece, mask)
        total = term if total is None else total + term
    return total


def pack_first(x_ref, b_ref, dt_ref, out_ref, steps, held, sems):
    count = out_ref.shape[0]
    heads_dev = dt_ref.shape[1] // count
    width = x_ref.shape[1] // count
    copies = []
    for d in range(count):
        copies.append(
            pltpu.make_async_copy(
                x_ref.at[:, d * width : (d + 1) * width],
                out_ref.at[d, :, 0:width],
                sems.at[0, d],
            )
        )
        copies.append(
            pltpu.make_async_copy(
                b_ref.at[:, d * STATE : (d + 1) * STATE],
                out_ref.at[d, :, width : width + STATE],
                sems.at[1, d],
            )
        )
    early = pltpu.make_async_copy(dt_ref, steps, sems.at[1, count])
    early.start()
    for copy in copies:
        copy.start()
    early.wait()
    raw = steps[...].astype(f32)
    raw = jnp.concatenate([raw, jnp.zeros((raw.shape[0], STATE - raw.shape[1]), f32)], axis=1)
    for d in range(count):
        mine = raw if d == 0 else pltpu.roll(raw, STATE - d * heads_dev, 1)
        held[d] = mine.astype(bf16)
    last = pltpu.make_async_copy(
        held, out_ref.at[:, :, width + STATE : width + 2 * STATE], sems.at[0, count]
    )
    last.start()
    for copy in copies:
        copy.wait()
    last.wait()


def pack_second(me_ref, after_ref, z_ref, c_ref, *refs):
    del after_ref
    out_refs, sems = refs[:-1], refs[-1]
    count = len(out_refs)
    width = z_ref.shape[1] // count
    copies = []
    for k in range(count):
        peer = me_ref[0] ^ k
        z_start = pl.multiple_of(peer * width, STATE)
        c_start = pl.multiple_of(peer * STATE, STATE)
        copies.append(
            pltpu.make_async_copy(
                z_ref.at[:, pl.ds(z_start, width)], out_refs[k].at[:, 0:width], sems.at[0, k]
            )
        )
        copies.append(
            pltpu.make_async_copy(
                c_ref.at[:, pl.ds(c_start, STATE)],
                out_refs[k].at[:, width : width + STATE],
                sems.at[1, k],
            )
        )
    for copy in copies:
        copy.start()
    for copy in copies:
        copy.wait()


def pack_cache(cache_ref, out_ref):
    for s in range(SLOTS):
        out_ref[:, s * STATE : (s + 1) * STATE] = cache_ref[s].astype(bf16)


def segment_of(position, ends):
    return (position >= ends[0]).astype(jnp.int32) + (position >= ends[1]).astype(jnp.int32)


def segment_ends(len_ref):
    first = len_ref[0, 0]
    return first, first + len_ref[0, 1]


def spread_heads(heads, width):
    row = lax.broadcasted_iota(jnp.int32, (heads, width), 0)
    column = lax.broadcasted_iota(jnp.int32, (heads, width), 1)
    return (row == column // (width // heads)).astype(bf16)


def local_state(len_ref, rate_ref, tok_ref, send_ref, out_ref):
    del send_ref
    length = tok_ref.shape[0]
    heads = rate_ref.shape[1]
    width = heads * HEAD_DIM
    ends = segment_ends(len_ref)
    step_size = jax.nn.softplus(tok_ref[:, width + STATE : width + STATE + heads].astype(f32))
    log_decay = -step_size * rate_ref[...]
    row = lax.broadcasted_iota(jnp.int32, (length, length), 0)
    column = lax.broadcasted_iota(jnp.int32, (length, length), 1)
    later = (segment_of(row, ends) == segment_of(column, ends)) & (column > row)
    after = exact_left(later.astype(f32).astype(bf16), log_decay)
    weight = exact_right(jnp.exp(after) * step_size, spread_heads(heads, width), 2)
    scaled = (weight * tok_ref[:, 0:width].astype(f32)).astype(bf16)
    token = lax.broadcasted_iota(jnp.int32, (length, STATE), 0)
    lane = lax.broadcasted_iota(jnp.int32, (length, STATE), 1)
    seg_index = segment_of(token, ends)
    b_half = tok_ref[:, width : width + STATE].astype(f32)
    b_parts = jnp.concatenate(
        [jnp.where(seg_index == j, b_half, 0.0).astype(bf16) for j in range(REQS)], axis=1
    )
    out_ref[:, 0 : REQS * STATE] = dot_tn(scaled, b_parts).astype(bf16)
    member = (seg_index == lane % REQS).astype(f32).astype(bf16)
    total = None
    for piece in split(log_decay, 3):
        term = dot_tn(piece, member)
        total = term if total is None else total + term
    kept = jnp.exp(total)
    high = kept.astype(bf16).astype(f32)
    lane_h = lax.broadcasted_iota(jnp.int32, (heads, STATE), 1)
    parts = jnp.where(lane_h < REQS, high, jnp.where(lane_h < 2 * REQS, kept - high, 0.0))
    row_w = lax.broadcasted_iota(jnp.int32, (width, heads), 0)
    col_w = lax.broadcasted_iota(jnp.int32, (width, heads), 1)
    owner = (row_w // HEAD_DIM == col_w).astype(f32).astype(bf16)
    spread = dot(owner, parts.astype(bf16))
    row_s = lax.broadcasted_iota(jnp.int32, (width, STATE), 0)
    lane_s = lax.broadcasted_iota(jnp.int32, (width, STATE), 1)
    chosen = jnp.where(lane_s == row_s % ROWS, spread, 0.0).astype(bf16)
    out_ref[:, REQS * STATE :] = dot(chosen, jnp.ones((STATE, STATE), bf16)).astype(bf16)


def combine(hit_ref, place_ref, after_ref, recv_ref, out_ref, held):
    del after_ref
    for s in range(recv_ref.shape[0]):
        block = recv_ref[s, :, 0 : SLOTS * STATE].astype(f32)
        for k in range(SLOTS):
            held[s * SLOTS + k] = block[:, k * STATE : (k + 1) * STATE]
    for s in range(recv_ref.shape[0]):
        block = recv_ref[s, :, SLOTS * STATE :].astype(f32)
        kept = block[:, REQS * STATE :]
        for j in range(REQS):
            prefix = held[hit_ref[s * REQS + j]]
            out_ref[s, :, j * STATE : (j + 1) * STATE] = prefix.astype(bf16)
            factor = kept[j : j + 1, :] + kept[REQS + j : REQS + j + 1, :]
            new = factor * prefix + block[:, j * STATE : (j + 1) * STATE]
            place = place_ref[s * REQS + j]
            start = pl.multiple_of((REQS + (place & 3)) * STATE, STATE)
            out_ref[place >> 2, :, pl.ds(start, STATE)] = new.astype(bf16)


def write_cache(missing_ref, cache_ref, recv_ref, out_ref):
    missing = missing_ref[0]
    for s in range(SLOTS):

        @pl.when(missing == s)
        def _():
            out_ref[s] = cache_ref[s]

        if s < REQS:

            @pl.when(missing > s)
            def _():
                out_ref[s] = recv_ref[:, (REQS + s) * STATE : (REQS + s + 1) * STATE].astype(f32)

        if s > 0:

            @pl.when(missing < s)
            def _():
                out_ref[s] = recv_ref[:, (REQS + s - 1) * STATE : (REQS + s) * STATE].astype(f32)


def token_inner(len_ref, me_ref, rate_ref, skip_ref, tok_ref, *refs):
    gate_refs, (base_ref, factor_ref, read_ref, gates, sems) = refs[:-5], refs[-5:]
    length = tok_ref.shape[0]
    heads = rate_ref.shape[1]
    width = heads * HEAD_DIM
    rows = length // len(gate_refs)
    copies = []
    for k in range(len(gate_refs)):
        start = pl.multiple_of((me_ref[0] ^ k) * rows, rows)
        copies.append(
            pltpu.make_async_copy(gate_refs[k], gates.at[pl.ds(start, rows), :], sems.at[k])
        )
    for copy in copies:
        copy.start()
    ends = segment_ends(len_ref)
    step_size = jax.nn.softplus(tok_ref[:, width + STATE : width + STATE + heads].astype(f32))
    log_decay = -step_size * rate_ref[...]
    row = lax.broadcasted_iota(jnp.int32, (length, length), 0)
    column = lax.broadcasted_iota(jnp.int32, (length, length), 1)
    upto = (segment_of(row, ends) == segment_of(column, ends)) & (column <= row)
    running = exact_left(upto.astype(f32).astype(bf16), log_decay)
    spread = spread_heads(heads, width)
    decay = exact_right(jnp.exp(running), spread)
    undo = exact_right(jnp.exp(-running) * step_size, spread, 2)
    values = tok_ref[:, 0:width].astype(f32)
    b_half = tok_ref[:, width : width + STATE]
    for copy in copies:
        copy.wait()
    c_half = gates[:, width : width + STATE]
    c_wide = c_half.astype(f32)
    scores = jnp.where(upto, dot_nt(c_half, b_half), 0.0).astype(bf16)
    token = lax.broadcasted_iota(jnp.int32, (length, STATE), 0)
    seg_index = segment_of(token, ends)
    for j in range(REQS):
        read_ref[:, j * STATE : (j + 1) * STATE] = jnp.where(seg_index == j, c_wide, 0.0).astype(
            bf16
        )
    inner = dot(scores, (undo * values).astype(bf16))
    gate_in = gates[:, 0:width].astype(f32)
    gate = gate_in / (1.0 + jnp.exp(-gate_in))
    base_ref[...] = gate * (decay * inner + exact_right(skip_ref[...], spread) * values)
    factor_ref[...] = gate * decay


def token_outputs(gain_ref, base_ref, factor_ref, read_ref, recv_ref, out_ref):
    carried = dot_nt(read_ref[...], recv_ref[:, 0 : REQS * STATE])
    gated = base_ref[...] + factor_ref[...] * carried
    square_mean = jnp.mean(gated * gated, axis=1, keepdims=True)
    out_ref[...] = (gated * lax.rsqrt(square_mean + 1e-05) * gain_ref[...]).astype(bf16)


def gated_norm(values, gate_in, norm_weight):
    shaped = values.shape
    gated = values * jax.nn.silu(gate_in.astype(jnp.float32).reshape(shaped))
    square_mean = jnp.mean(gated * gated, axis=(2, 3), keepdims=True)
    normed = gated * lax.rsqrt(square_mean + 1e-05) * norm_weight.reshape(shaped[1:])
    return normed.reshape(shaped[0], -1).astype(jnp.bfloat16)


def decode_block(
    inputs, gate_in, b_proj, c_proj, step_raw, states, head_rates, skip_gain, norm_weight
):
    row_count = inputs.shape[0]
    head_count = step_raw.shape[1]
    groups = b_proj.shape[1] // STATE
    per_group = head_count // groups
    step_size = jax.nn.softplus(step_raw.astype(jnp.float32))
    factor = jnp.exp(-step_size * head_rates[None, :]).reshape(row_count, groups, per_group, 1, 1)
    values = inputs.astype(jnp.float32).reshape(row_count, groups, per_group, HEAD_DIM)
    b_group = b_proj.astype(jnp.float32).reshape(row_count, groups, STATE)
    c_group = c_proj.astype(jnp.float32).reshape(row_count, groups, STATE)
    written = (step_size.reshape(row_count, groups, per_group, 1) * values)[..., None] * b_group[
        :, :, None, None, :
    ]
    updated = factor * states.reshape(row_count, groups, per_group, HEAD_DIM, STATE) + written
    outputs = (
        jnp.einsum("rgkpn,rgn->rgkp", updated, c_group, precision=highest)
        + skip_gain.reshape(groups, per_group, 1) * values
    )
    return (
        gated_norm(outputs, gate_in, norm_weight),
        updated.reshape(row_count, head_count, HEAD_DIM, STATE),
    )


def local(
    pre_x,
    pre_z,
    pre_b,
    pre_c,
    pre_dt,
    suffix_lengths,
    prefix_hits,
    snapshot_slots,
    cache_states,
    dec_x,
    dec_z,
    dec_b,
    dec_c,
    dec_dt,
    dec_states,
    decay_rate,
    d_skip,
    norm_weight,
):
    n_head = lax.axis_size("head")
    n_serve = lax.axis_size("serve")
    rows = pre_x.shape[0]
    heads = cache_states.shape[1]
    width = heads * HEAD_DIM
    length = rows * n_head
    tiles = SLOTS + REQS + 1
    shape = jax.ShapeDtypeStruct

    def swap(value, axis):
        return lax.all_to_all(value, axis, split_axis=0, concat_axis=0, tiled=True)

    with jax.named_scope("tokens"):
        first = pl.pallas_call(
            pack_first,
            out_shape=shape((n_head, rows, width + 2 * STATE), bf16),
            in_specs=[HBM] * 3,
            out_specs=HBM,
            scratch_shapes=[
                pltpu.VMEM(pre_dt.shape, bf16),
                pltpu.VMEM((n_head, rows, STATE), bf16),
                pltpu.SemaphoreType.DMA((2, n_head + 1)),
            ],
            compiler_params=params(),
            cost_estimate=cost(0, 800_000),
        )(pre_x, pre_b, pre_dt)
        tokens = swap(first, "head").reshape(length, width + 2 * STATE)
    with jax.named_scope("cache"):
        cache_rows = cache_states.reshape(SLOTS, width, STATE)
        send = pl.pallas_call(
            pack_cache,
            out_shape=shape((width, tiles * STATE), bf16),
            grid=(1,),
            in_specs=[VMEM],
            out_specs=pl.BlockSpec((width, SLOTS * STATE), lambda i: (0, 0)),
            compiler_params=params(),
            cost_estimate=cost(0, 1_600_000),
        )(cache_rows)
    with jax.named_scope("orders"):
        rank = jnp.sum(
            (snapshot_slots[None, :] < snapshot_slots[:, None]).astype(jnp.int32), axis=1
        )
        place = (rank // REQS) * 4 + rank % REQS
        serve_me = lax.axis_index("serve")
        missing = (
            sum(range(SLOTS))
            - jnp.sum(jnp.where(snapshot_slots // SLOTS == serve_me, snapshot_slots % SLOTS, 0))
        ).reshape(1)
        head_me = lax.axis_index("head").astype(jnp.int32).reshape(1)
    rates = decay_rate.reshape(1, heads)
    with jax.named_scope("local"):
        send = pl.pallas_call(
            local_state,
            out_shape=shape((width, tiles * STATE), bf16),
            grid=(1,),
            in_specs=[SMEM, VMEM, VMEM, ANY],
            out_specs=pl.BlockSpec((width, SLOTS * STATE), lambda i: (0, 1)),
            input_output_aliases={3: 0},
            compiler_params=params(),
            cost_estimate=cost(300_000_000, 800_000),
        )(suffix_lengths, rates, tokens, send)
        pieces = swap(send.reshape(n_serve, ROWS, tiles * STATE), "serve")
    with jax.named_scope("gates"):
        mine = pl.pallas_call(
            pack_second,
            out_shape=[shape((rows, width + STATE), bf16)] * n_head,
            in_specs=[SMEM, ANY, HBM, HBM],
            out_specs=[ANY] * n_head,
            scratch_shapes=[pltpu.SemaphoreType.DMA((2, n_head))],
            compiler_params=params(),
            cost_estimate=cost(0, 650_000),
        )(head_me, send, pre_z, pre_c)
        gates = [mine[0]] + [
            lax.ppermute(mine[k], "head", [(i, i ^ k) for i in range(n_head)])
            for k in range(1, n_head)
        ]
    with jax.named_scope("inner"):
        base, factor, read = pl.pallas_call(
            token_inner,
            out_shape=(
                shape((length, width), f32),
                shape((length, width), f32),
                shape((length, REQS * STATE), bf16),
            ),
            in_specs=[SMEM] * 2 + [VMEM] * 3 + [ANY] * n_head,
            out_specs=[VMEM] * 3,
            scratch_shapes=[
                pltpu.VMEM((length, width + STATE), bf16),
                pltpu.SemaphoreType.DMA((n_head,)),
            ],
            compiler_params=params(),
            cost_estimate=cost(400_000_000, 1_500_000),
        )(suffix_lengths, head_me, rates, d_skip.reshape(1, heads), tokens, *gates)
    with jax.named_scope("combine"):
        answer = pl.pallas_call(
            combine,
            out_shape=shape((n_serve, ROWS, 2 * REQS * STATE), bf16),
            in_specs=[SMEM, SMEM, ANY, VMEM],
            out_specs=VMEM,
            scratch_shapes=[pltpu.VMEM((n_serve * SLOTS, ROWS, STATE), f32)],
            compiler_params=params(),
            cost_estimate=cost(0, 4_000_000),
        )(prefix_hits, place, read, pieces)
        got = swap(answer, "serve").reshape(width, 2 * REQS * STATE)
    dec_out, dec_new = decode_block(
        dec_x, dec_z, dec_b, dec_c, dec_dt, dec_states, decay_rate, d_skip, norm_weight
    )
    with jax.named_scope("outputs"):
        pre_out = pl.pallas_call(
            token_outputs,
            out_shape=shape((length, width), bf16),
            in_specs=[VMEM] * 5,
            out_specs=VMEM,
            compiler_params=params(),
            cost_estimate=cost(200_000_000, 1_500_000),
        )(norm_weight.reshape(1, width), base, factor, read, got)
        cache_out = pl.pallas_call(
            write_cache,
            out_shape=shape((SLOTS, width, STATE), f32),
            in_specs=[SMEM, VMEM, VMEM],
            out_specs=VMEM,
            compiler_params=params(),
            cost_estimate=cost(0, 2_500_000),
        )(missing, cache_rows, got).reshape(cache_states.shape)
    return (pre_out, cache_out, dec_out, dec_new)


def solution(mesh):
    return jax.shard_map(
        local,
        mesh=mesh,
        in_specs=(
            P(("serve", "head"), None),
            P(("serve", "head"), None),
            P(("serve", "head"), None),
            P(("serve", "head"), None),
            P(("serve", "head"), None),
            P("serve", None),
            P(),
            P(),
            P("serve", "head", None, None),
            P("serve", "head"),
            P("serve", "head"),
            P("serve", "head"),
            P("serve", "head"),
            P("serve", "head"),
            P("serve", "head", None, None),
            P("head"),
            P("head"),
            P("head"),
        ),
        out_specs=(
            P("serve", "head"),
            P("serve", "head", None, None),
            P("serve", "head"),
            P("serve", "head", None, None),
        ),
        check_vma=False,
    )
```

```python
import jax
import jax.numpy as jnp
from jax import lax
from jax.experimental import pallas as pl
from jax.experimental.pallas import tpu as pltpu
from jax.sharding import PartitionSpec as P

HEAD_DIM = 64
STATE = 128
REQS = 3
SLOTS = 4
ROWS = 8
STRIDE = 37

f32 = jnp.float32
bf16 = jnp.bfloat16
highest = lax.Precision.HIGHEST

ANY = pl.BlockSpec(memory_space=pl.ANY)
HBM = pl.BlockSpec(memory_space=pltpu.HBM)
VMEM = pl.BlockSpec(memory_space=pltpu.VMEM)
SMEM = pl.BlockSpec(memory_space=pltpu.SMEM)


def params(mib=12):
    return pltpu.CompilerParams(vmem_limit_bytes=mib * 1024 * 1024)


def cost(flops, moved):
    return pl.CostEstimate(flops=flops, bytes_accessed=moved, transcendentals=0)


def dot(a, b):
    return jnp.dot(a, b, preferred_element_type=f32)


def dot_nt(a, b):
    return lax.dot_general(a, b, (((1,), (1,)), ((), ())), preferred_element_type=f32)


def dot_tn(a, b):
    return lax.dot_general(a, b, (((0,), (0,)), ((), ())), preferred_element_type=f32)


def split(value, parts):
    pieces = []
    for _ in range(parts):
        piece = value.astype(bf16)
        pieces.append(piece)
        value = value - piece.astype(f32)
    return pieces


def exact_left(mask, value, parts=3):
    total = None
    for piece in split(value, parts):
        term = dot(mask, piece)
        total = term if total is None else total + term
    return total


def exact_right(value, mask, parts=3):
    total = None
    for piece in split(value, parts):
        term = dot(piece, mask)
        total = term if total is None else total + term
    return total


def pack_first(x_ref, b_ref, dt_ref, out_ref, steps, held, sems):
    count = out_ref.shape[0]
    heads_dev = dt_ref.shape[1] // count
    width = x_ref.shape[1] // count
    copies = []
    for d in range(count):
        copies.append(
            pltpu.make_async_copy(
                x_ref.at[:, d * width : (d + 1) * width],
                out_ref.at[d, :, 0:width],
                sems.at[0, d],
            )
        )
        copies.append(
            pltpu.make_async_copy(
                b_ref.at[:, d * STATE : (d + 1) * STATE],
                out_ref.at[d, :, width : width + STATE],
                sems.at[1, d],
            )
        )
    early = pltpu.make_async_copy(dt_ref, steps, sems.at[1, count])
    early.start()
    for copy in copies:
        copy.start()
    early.wait()
    raw = steps[...].astype(f32)
    raw = jnp.concatenate([raw, jnp.zeros((raw.shape[0], STATE - raw.shape[1]), f32)], axis=1)
    for d in range(count):
        mine = raw if d == 0 else pltpu.roll(raw, STATE - d * heads_dev, 1)
        held[d] = mine.astype(bf16)
    last = pltpu.make_async_copy(
        held, out_ref.at[:, :, width + STATE : width + 2 * STATE], sems.at[0, count]
    )
    last.start()
    for copy in copies:
        copy.wait()
    last.wait()


def pack_second(me_ref, after_ref, z_ref, c_ref, *refs):
    del after_ref
    out_refs, sems = refs[:-1], refs[-1]
    count = len(out_refs)
    width = z_ref.shape[1] // count
    copies = []
    for k in range(count):
        peer = me_ref[0] ^ k
        z_start = pl.multiple_of(peer * width, STATE)
        c_start = pl.multiple_of(peer * STATE, STATE)
        copies.append(
            pltpu.make_async_copy(
                z_ref.at[:, pl.ds(z_start, width)], out_refs[k].at[:, 0:width], sems.at[0, k]
            )
        )
        copies.append(
            pltpu.make_async_copy(
                c_ref.at[:, pl.ds(c_start, STATE)],
                out_refs[k].at[:, width : width + STATE],
                sems.at[1, k],
            )
        )
    for copy in copies:
        copy.start()
    for copy in copies:
        copy.wait()


def pack_cache(cache_ref, out_ref):
    for s in range(SLOTS):
        out_ref[:, s * STATE : (s + 1) * STATE] = cache_ref[s].astype(bf16)


def segment_of(position, ends):
    return (position >= ends[0]).astype(jnp.int32) + (position >= ends[1]).astype(jnp.int32)


def segment_ends(len_ref):
    first = len_ref[0, 0]
    return first, first + len_ref[0, 1]


def spread_heads(heads, width):
    row = lax.broadcasted_iota(jnp.int32, (heads, width), 0)
    column = lax.broadcasted_iota(jnp.int32, (heads, width), 1)
    return (row == column // (width // heads)).astype(bf16)


def local_state(len_ref, rate_ref, tok_ref, send_ref, out_ref):
    del send_ref
    length = tok_ref.shape[0]
    heads = rate_ref.shape[1]
    width = heads * HEAD_DIM
    ends = segment_ends(len_ref)
    step_size = jax.nn.softplus(tok_ref[:, width + STATE : width + STATE + heads].astype(f32))
    log_decay = -step_size * rate_ref[...]
    row = lax.broadcasted_iota(jnp.int32, (length, length), 0)
    column = lax.broadcasted_iota(jnp.int32, (length, length), 1)
    later = (segment_of(row, ends) == segment_of(column, ends)) & (column > row)
    after = exact_left(later.astype(f32).astype(bf16), log_decay)
    weight = exact_right(jnp.exp(after) * step_size, spread_heads(heads, width), 2)
    scaled = (weight * tok_ref[:, 0:width].astype(f32)).astype(bf16)
    token = lax.broadcasted_iota(jnp.int32, (length, STATE), 0)
    lane = lax.broadcasted_iota(jnp.int32, (length, STATE), 1)
    seg_index = segment_of(token, ends)
    b_half = tok_ref[:, width : width + STATE].astype(f32)
    b_parts = jnp.concatenate(
        [jnp.where(seg_index == j, b_half, 0.0).astype(bf16) for j in range(REQS)], axis=1
    )
    out_ref[:, 0 : REQS * STATE] = dot_tn(scaled, b_parts).astype(bf16)
    member = (seg_index == lane % REQS).astype(f32).astype(bf16)
    total = None
    for piece in split(log_decay, 3):
        term = dot_tn(piece, member)
        total = term if total is None else total + term
    kept = jnp.exp(total)
    high = kept.astype(bf16).astype(f32)
    lane_h = lax.broadcasted_iota(jnp.int32, (heads, STATE), 1)
    parts = jnp.where(lane_h < REQS, high, jnp.where(lane_h < 2 * REQS, kept - high, 0.0))
    row_w = lax.broadcasted_iota(jnp.int32, (width, heads), 0)
    col_w = lax.broadcasted_iota(jnp.int32, (width, heads), 1)
    owner = (row_w // HEAD_DIM == col_w).astype(f32).astype(bf16)
    spread = dot(owner, parts.astype(bf16))
    row_s = lax.broadcasted_iota(jnp.int32, (width, STATE), 0)
    lane_s = lax.broadcasted_iota(jnp.int32, (width, STATE), 1)
    chosen = jnp.where(lane_s == row_s % ROWS, spread, 0.0).astype(bf16)
    out_ref[:, REQS * STATE :] = dot(chosen, jnp.ones((STATE, STATE), bf16)).astype(bf16)


def partners(count):
    return [i * STRIDE % count for i in range(count)]


def combine(hit_ref, place_ref, after_ref, recv_ref, out_ref, held):
    del after_ref
    order = partners(recv_ref.shape[0])
    for i, s in enumerate(order):
        block = recv_ref[i, :, 0 : SLOTS * STATE].astype(f32)
        for k in range(SLOTS):
            held[s * SLOTS + k] = block[:, k * STATE : (k + 1) * STATE]
    for i, s in enumerate(order):
        block = recv_ref[i, :, SLOTS * STATE :].astype(f32)
        kept = block[:, REQS * STATE :]
        for j in range(REQS):
            prefix = held[hit_ref[s * REQS + j]]
            out_ref[i, :, j * STATE : (j + 1) * STATE] = prefix.astype(bf16)
            factor = kept[j : j + 1, :] + kept[REQS + j : REQS + j + 1, :]
            new = factor * prefix + block[:, j * STATE : (j + 1) * STATE]
            place = place_ref[s * REQS + j]
            start = pl.multiple_of((REQS + (place & 3)) * STATE, STATE)
            out_ref[place >> 2, :, pl.ds(start, STATE)] = new.astype(bf16)


def write_cache(missing_ref, cache_ref, recv_ref, out_ref):
    missing = missing_ref[0]
    for s in range(SLOTS):

        @pl.when(missing == s)
        def _():
            out_ref[s] = cache_ref[s]

        if s < REQS:

            @pl.when(missing > s)
            def _():
                out_ref[s] = recv_ref[:, (REQS + s) * STATE : (REQS + s + 1) * STATE].astype(f32)

        if s > 0:

            @pl.when(missing < s)
            def _():
                out_ref[s] = recv_ref[:, (REQS + s - 1) * STATE : (REQS + s) * STATE].astype(f32)


def token_inner(len_ref, me_ref, rate_ref, skip_ref, tok_ref, *refs):
    gate_refs, (base_ref, factor_ref, read_ref, gates, sems) = refs[:-5], refs[-5:]
    length = tok_ref.shape[0]
    heads = rate_ref.shape[1]
    width = heads * HEAD_DIM
    rows = length // len(gate_refs)
    copies = []
    for k in range(len(gate_refs)):
        start = pl.multiple_of((me_ref[0] ^ k) * rows, rows)
        copies.append(
            pltpu.make_async_copy(gate_refs[k], gates.at[pl.ds(start, rows), :], sems.at[k])
        )
    for copy in copies:
        copy.start()
    ends = segment_ends(len_ref)
    step_size = jax.nn.softplus(tok_ref[:, width + STATE : width + STATE + heads].astype(f32))
    log_decay = -step_size * rate_ref[...]
    row = lax.broadcasted_iota(jnp.int32, (length, length), 0)
    column = lax.broadcasted_iota(jnp.int32, (length, length), 1)
    upto = (segment_of(row, ends) == segment_of(column, ends)) & (column <= row)
    running = exact_left(upto.astype(f32).astype(bf16), log_decay)
    spread = spread_heads(heads, width)
    decay = exact_right(jnp.exp(running), spread)
    undo = exact_right(jnp.exp(-running) * step_size, spread, 2)
    values = tok_ref[:, 0:width].astype(f32)
    b_half = tok_ref[:, width : width + STATE]
    for copy in copies:
        copy.wait()
    c_half = gates[:, width : width + STATE]
    c_wide = c_half.astype(f32)
    scores = jnp.where(upto, dot_nt(c_half, b_half), 0.0).astype(bf16)
    token = lax.broadcasted_iota(jnp.int32, (length, STATE), 0)
    seg_index = segment_of(token, ends)
    for j in range(REQS):
        read_ref[:, j * STATE : (j + 1) * STATE] = jnp.where(seg_index == j, c_wide, 0.0).astype(
            bf16
        )
    inner = dot(scores, (undo * values).astype(bf16))
    gate_in = gates[:, 0:width].astype(f32)
    gate = gate_in / (1.0 + jnp.exp(-gate_in))
    base_ref[...] = gate * (decay * inner + exact_right(skip_ref[...], spread) * values)
    factor_ref[...] = gate * decay


def token_outputs(gain_ref, base_ref, factor_ref, read_ref, recv_ref, out_ref):
    carried = dot_nt(read_ref[...], recv_ref[:, 0 : REQS * STATE])
    gated = base_ref[...] + factor_ref[...] * carried
    square_mean = jnp.mean(gated * gated, axis=1, keepdims=True)
    out_ref[...] = (gated * lax.rsqrt(square_mean + 1e-05) * gain_ref[...]).astype(bf16)


def gated_norm(values, gate_in, norm_weight):
    shaped = values.shape
    gated = values * jax.nn.silu(gate_in.astype(jnp.float32).reshape(shaped))
    square_mean = jnp.mean(gated * gated, axis=(2, 3), keepdims=True)
    normed = gated * lax.rsqrt(square_mean + 1e-05) * norm_weight.reshape(shaped[1:])
    return normed.reshape(shaped[0], -1).astype(jnp.bfloat16)


def decode_block(
    inputs, gate_in, b_proj, c_proj, step_raw, states, head_rates, skip_gain, norm_weight
):
    row_count = inputs.shape[0]
    head_count = step_raw.shape[1]
    groups = b_proj.shape[1] // STATE
    per_group = head_count // groups
    step_size = jax.nn.softplus(step_raw.astype(jnp.float32))
    factor = jnp.exp(-step_size * head_rates[None, :]).reshape(row_count, groups, per_group, 1, 1)
    values = inputs.astype(jnp.float32).reshape(row_count, groups, per_group, HEAD_DIM)
    b_group = b_proj.astype(jnp.float32).reshape(row_count, groups, STATE)
    c_group = c_proj.astype(jnp.float32).reshape(row_count, groups, STATE)
    written = (step_size.reshape(row_count, groups, per_group, 1) * values)[..., None] * b_group[
        :, :, None, None, :
    ]
    updated = factor * states.reshape(row_count, groups, per_group, HEAD_DIM, STATE) + written
    outputs = (
        jnp.einsum("rgkpn,rgn->rgkp", updated, c_group, precision=highest)
        + skip_gain.reshape(groups, per_group, 1) * values
    )
    return (
        gated_norm(outputs, gate_in, norm_weight),
        updated.reshape(row_count, head_count, HEAD_DIM, STATE),
    )


def local(
    pre_x,
    pre_z,
    pre_b,
    pre_c,
    pre_dt,
    suffix_lengths,
    prefix_hits,
    snapshot_slots,
    cache_states,
    dec_x,
    dec_z,
    dec_b,
    dec_c,
    dec_dt,
    dec_states,
    decay_rate,
    d_skip,
    norm_weight,
):
    n_head = lax.axis_size("head")
    n_serve = lax.axis_size("serve")
    rows = pre_x.shape[0]
    heads = cache_states.shape[1]
    width = heads * HEAD_DIM
    length = rows * n_head
    tiles = SLOTS + REQS + 1
    shape = jax.ShapeDtypeStruct

    def swap(value, axis):
        groups = [partners(n_serve)] if axis == "serve" else None
        return lax.all_to_all(
            value, axis, split_axis=0, concat_axis=0, tiled=True, axis_index_groups=groups
        )

    with jax.named_scope("tokens"):
        first = pl.pallas_call(
            pack_first,
            out_shape=shape((n_head, rows, width + 2 * STATE), bf16),
            in_specs=[HBM] * 3,
            out_specs=HBM,
            scratch_shapes=[
                pltpu.VMEM(pre_dt.shape, bf16),
                pltpu.VMEM((n_head, rows, STATE), bf16),
                pltpu.SemaphoreType.DMA((2, n_head + 1)),
            ],
            compiler_params=params(56),
            cost_estimate=cost(0, 800_000),
        )(pre_x, pre_b, pre_dt)
        tokens = swap(first, "head").reshape(length, width + 2 * STATE)
    with jax.named_scope("cache"):
        cache_rows = cache_states.reshape(SLOTS, width, STATE)
        send = pl.pallas_call(
            pack_cache,
            out_shape=shape((width, tiles * STATE), bf16),
            grid=(1,),
            in_specs=[VMEM],
            out_specs=pl.BlockSpec((width, SLOTS * STATE), lambda i: (0, 0)),
            compiler_params=params(),
            cost_estimate=cost(0, 1_600_000),
        )(cache_rows)
    with jax.named_scope("orders"):
        rank = jnp.sum(
            (snapshot_slots[None, :] < snapshot_slots[:, None]).astype(jnp.int32), axis=1
        )
        seat = (rank // REQS) * pow(STRIDE, -1, n_serve) % n_serve
        place = seat * 4 + rank % REQS
        serve_me = lax.axis_index("serve")
        missing = (
            sum(range(SLOTS))
            - jnp.sum(jnp.where(snapshot_slots // SLOTS == serve_me, snapshot_slots % SLOTS, 0))
        ).reshape(1)
        head_me = lax.axis_index("head").astype(jnp.int32).reshape(1)
    rates = decay_rate.reshape(1, heads)
    with jax.named_scope("local"):
        send = pl.pallas_call(
            local_state,
            out_shape=shape((width, tiles * STATE), bf16),
            grid=(1,),
            in_specs=[SMEM, VMEM, VMEM, ANY],
            out_specs=pl.BlockSpec((width, SLOTS * STATE), lambda i: (0, 1)),
            input_output_aliases={3: 0},
            compiler_params=params(),
            cost_estimate=cost(300_000_000, 800_000),
        )(suffix_lengths, rates, tokens, send)
        pieces = swap(send.reshape(n_serve, ROWS, tiles * STATE), "serve")
    with jax.named_scope("gates"):
        mine = pl.pallas_call(
            pack_second,
            out_shape=[shape((rows, width + STATE), bf16)] * n_head,
            in_specs=[SMEM, ANY, HBM, HBM],
            out_specs=[ANY] * n_head,
            scratch_shapes=[pltpu.SemaphoreType.DMA((2, n_head))],
            compiler_params=params(),
            cost_estimate=cost(0, 650_000),
        )(head_me, send, pre_z, pre_c)
        gates = [mine[0]] + [
            lax.ppermute(mine[k], "head", [(i, i ^ k) for i in range(n_head)])
            for k in range(1, n_head)
        ]
    with jax.named_scope("inner"):
        base, factor, read = pl.pallas_call(
            token_inner,
            out_shape=(
                shape((length, width), f32),
                shape((length, width), f32),
                shape((length, REQS * STATE), bf16),
            ),
            in_specs=[SMEM] * 2 + [VMEM] * 3 + [ANY] * n_head,
            out_specs=[VMEM] * 3,
            scratch_shapes=[
                pltpu.VMEM((length, width + STATE), bf16),
                pltpu.SemaphoreType.DMA((n_head,)),
            ],
            compiler_params=params(),
            cost_estimate=cost(400_000_000, 1_500_000),
        )(suffix_lengths, head_me, rates, d_skip.reshape(1, heads), tokens, *gates)
    with jax.named_scope("combine"):
        answer = pl.pallas_call(
            combine,
            out_shape=shape((n_serve, ROWS, 2 * REQS * STATE), bf16),
            in_specs=[SMEM, SMEM, ANY, VMEM],
            out_specs=VMEM,
            scratch_shapes=[pltpu.VMEM((n_serve * SLOTS, ROWS, STATE), f32)],
            compiler_params=params(),
            cost_estimate=cost(0, 4_000_000),
        )(prefix_hits, place, read, pieces)
        got = swap(answer, "serve").reshape(width, 2 * REQS * STATE)
    dec_out, dec_new = decode_block(
        dec_x, dec_z, dec_b, dec_c, dec_dt, dec_states, decay_rate, d_skip, norm_weight
    )
    with jax.named_scope("outputs"):
        pre_out = pl.pallas_call(
            token_outputs,
            out_shape=shape((length, width), bf16),
            in_specs=[VMEM] * 5,
            out_specs=VMEM,
            compiler_params=params(),
            cost_estimate=cost(200_000_000, 1_500_000),
        )(norm_weight.reshape(1, width), base, factor, read, got)
        cache_out = pl.pallas_call(
            write_cache,
            out_shape=shape((SLOTS, width, STATE), f32),
            in_specs=[SMEM, VMEM, VMEM],
            out_specs=VMEM,
            compiler_params=params(),
            cost_estimate=cost(0, 2_500_000),
        )(missing, cache_rows, got).reshape(cache_states.shape)
    return (pre_out, cache_out, dec_out, dec_new)


def solution(mesh):
    return jax.shard_map(
        local,
        mesh=mesh,
        in_specs=(
            P(("serve", "head"), None),
            P(("serve", "head"), None),
            P(("serve", "head"), None),
            P(("serve", "head"), None),
            P(("serve", "head"), None),
            P("serve", None),
            P(),
            P(),
            P("serve", "head", None, None),
            P("serve", "head"),
            P("serve", "head"),
            P("serve", "head"),
            P("serve", "head"),
            P("serve", "head"),
            P("serve", "head", None, None),
            P("head"),
            P("head"),
            P("head"),
        ),
        out_specs=(
            P("serve", "head"),
            P("serve", "head", None, None),
            P("serve", "head"),
            P("serve", "head", None, None),
        ),
        check_vma=False,
    )
```

```python
import jax
import jax.numpy as jnp
from jax import lax
from jax.experimental import pallas as pl
from jax.experimental.pallas import tpu as pltpu
from jax.sharding import PartitionSpec as P

HEAD_DIM = 64
STATE = 128
REQS = 3
SLOTS = 4
ROWS = 8

f32 = jnp.float32
bf16 = jnp.bfloat16
highest = lax.Precision.HIGHEST

ANY = pl.BlockSpec(memory_space=pl.ANY)
HBM = pl.BlockSpec(memory_space=pltpu.HBM)
VMEM = pl.BlockSpec(memory_space=pltpu.VMEM)
SMEM = pl.BlockSpec(memory_space=pltpu.SMEM)


def params(mib=12):
    return pltpu.CompilerParams(vmem_limit_bytes=mib * 1024 * 1024)


def cost(flops, moved):
    return pl.CostEstimate(flops=flops, bytes_accessed=moved, transcendentals=0)


def dot(a, b):
    return jnp.dot(a, b, preferred_element_type=f32)


def dot_nt(a, b):
    return lax.dot_general(a, b, (((1,), (1,)), ((), ())), preferred_element_type=f32)


def dot_tn(a, b):
    return lax.dot_general(a, b, (((0,), (0,)), ((), ())), preferred_element_type=f32)


def split(value, parts):
    pieces = []
    for _ in range(parts):
        piece = value.astype(bf16)
        pieces.append(piece)
        value = value - piece.astype(f32)
    return pieces


def exact_left(mask, value, parts=3):
    total = None
    for piece in split(value, parts):
        term = dot(mask, piece)
        total = term if total is None else total + term
    return total


def exact_right(value, mask, parts=3):
    total = None
    for piece in split(value, parts):
        term = dot(piece, mask)
        total = term if total is None else total + term
    return total


def pack_tokens(me_ref, after_ref, x_ref, b_ref, dt_ref, keep_ref, give_ref):
    del after_ref
    chips = keep_ref.shape[0]
    heads_dev = dt_ref.shape[1] // (2 * chips)
    width = x_ref.shape[1] // (2 * chips)
    raw = dt_ref[...].astype(f32)
    raw = jnp.concatenate([raw, jnp.zeros((raw.shape[0], STATE - raw.shape[1]), f32)], axis=1)
    for side, ref in enumerate((keep_ref, give_ref)):
        for k in range(chips):
            peer = me_ref[0] ^ (2 * k + side)
            x_start = pl.multiple_of(peer * width, STATE)
            b_start = pl.multiple_of(peer * STATE, STATE)
            ref[k, :, 0:width] = x_ref[:, pl.ds(x_start, width)]
            ref[k, :, width : width + STATE] = b_ref[:, pl.ds(b_start, STATE)]
            mine = pltpu.roll(raw, (STATE - peer * heads_dev) % STATE, 1)
            ref[k, :, width + STATE : width + 2 * STATE] = mine.astype(bf16)


def pack_gates(me_ref, after_ref, z_ref, c_ref, keep_ref, give_ref):
    del after_ref
    chips = keep_ref.shape[0]
    width = z_ref.shape[1] // (2 * chips)
    for side, ref in enumerate((keep_ref, give_ref)):
        for k in range(chips):
            peer = me_ref[0] ^ (2 * k + side)
            z_start = pl.multiple_of(peer * width, STATE)
            c_start = pl.multiple_of(peer * STATE, STATE)
            ref[k, :, 0:width] = z_ref[:, pl.ds(z_start, width)]
            ref[k, :, width : width + STATE] = c_ref[:, pl.ds(c_start, STATE)]


def pair_up(keep_ref, got_ref, *out_refs):
    for k, ref in enumerate(out_refs):
        ref[0] = keep_ref[k]
        ref[1] = got_ref[k]


def exchange(keep, give, n_head):
    chips = n_head // 2
    shape = jax.ShapeDtypeStruct((2,) + keep.shape[1:], bf16)
    got = lax.ppermute(give, "head", [(i, i ^ 1) for i in range(n_head)])
    pairs = pl.pallas_call(
        pair_up,
        out_shape=[shape] * chips,
        in_specs=[VMEM] * 2,
        out_specs=[VMEM] * chips,
        compiler_params=params(),
        cost_estimate=cost(0, 800_000),
    )(keep, got)
    return [pairs[0]] + [
        lax.ppermute(pairs[k], "head", [(i, i ^ (2 * k)) for i in range(n_head)])
        for k in range(1, chips)
    ]


def fetch(me, pair_refs, rows_ref, sems):
    rows = pair_refs[0].shape[1]
    copies = []
    for k, ref in enumerate(pair_refs):
        for side in range(2):
            start = pl.multiple_of((me ^ (2 * k + side)) * rows, rows)
            copies.append(
                pltpu.make_async_copy(
                    ref.at[side], rows_ref.at[pl.ds(start, rows), :], sems.at[2 * k + side]
                )
            )
    for copy in copies:
        copy.start()
    return copies


def pack_cache(cache_ref, out_ref):
    for s in range(SLOTS):
        out_ref[:, s * STATE : (s + 1) * STATE] = cache_ref[s].astype(bf16)


def segment_of(position, ends):
    return (position >= ends[0]).astype(jnp.int32) + (position >= ends[1]).astype(jnp.int32)


def segment_ends(len_ref):
    first = len_ref[0, 0]
    return first, first + len_ref[0, 1]


def spread_heads(heads, width):
    row = lax.broadcasted_iota(jnp.int32, (heads, width), 0)
    column = lax.broadcasted_iota(jnp.int32, (heads, width), 1)
    return (row == column // (width // heads)).astype(bf16)


def local_state(len_ref, me_ref, rate_ref, *refs):
    pair_refs, (send_ref, out_ref, tok_ref, made, sems, last_sem) = refs[:-6], refs[-6:]
    del send_ref
    length = tok_ref.shape[0]
    heads = rate_ref.shape[1]
    width = heads * HEAD_DIM
    for copy in fetch(me_ref[0], pair_refs, tok_ref, sems):
        copy.wait()
    ends = segment_ends(len_ref)
    step_size = jax.nn.softplus(tok_ref[:, width + STATE : width + STATE + heads].astype(f32))
    log_decay = -step_size * rate_ref[...]
    row = lax.broadcasted_iota(jnp.int32, (length, length), 0)
    column = lax.broadcasted_iota(jnp.int32, (length, length), 1)
    later = (segment_of(row, ends) == segment_of(column, ends)) & (column > row)
    after = exact_left(later.astype(f32).astype(bf16), log_decay)
    weight = exact_right(jnp.exp(after) * step_size, spread_heads(heads, width), 2)
    scaled = (weight * tok_ref[:, 0:width].astype(f32)).astype(bf16)
    token = lax.broadcasted_iota(jnp.int32, (length, STATE), 0)
    lane = lax.broadcasted_iota(jnp.int32, (length, STATE), 1)
    seg_index = segment_of(token, ends)
    b_half = tok_ref[:, width : width + STATE].astype(f32)
    b_parts = jnp.concatenate(
        [jnp.where(seg_index == j, b_half, 0.0).astype(bf16) for j in range(REQS)], axis=1
    )
    made[:, 0 : REQS * STATE] = dot_tn(scaled, b_parts).astype(bf16)
    member = (seg_index == lane % REQS).astype(f32).astype(bf16)
    total = None
    for piece in split(log_decay, 3):
        term = dot_tn(piece, member)
        total = term if total is None else total + term
    kept = jnp.exp(total)
    high = kept.astype(bf16).astype(f32)
    lane_h = lax.broadcasted_iota(jnp.int32, (heads, STATE), 1)
    parts = jnp.where(lane_h < REQS, high, jnp.where(lane_h < 2 * REQS, kept - high, 0.0))
    row_w = lax.broadcasted_iota(jnp.int32, (width, heads), 0)
    col_w = lax.broadcasted_iota(jnp.int32, (width, heads), 1)
    owner = (row_w // HEAD_DIM == col_w).astype(f32).astype(bf16)
    spread = dot(owner, parts.astype(bf16))
    row_s = lax.broadcasted_iota(jnp.int32, (width, STATE), 0)
    lane_s = lax.broadcasted_iota(jnp.int32, (width, STATE), 1)
    chosen = jnp.where(lane_s == row_s % ROWS, spread, 0.0).astype(bf16)
    made[:, REQS * STATE :] = dot(chosen, jnp.ones((STATE, STATE), bf16)).astype(bf16)
    last = pltpu.make_async_copy(made, out_ref.at[:, REQS * STATE :], last_sem)
    last.start()
    last.wait()


def pick_prefix(hit_ref, recv_ref, out_ref, picked_ref, held, sem):
    for s in range(recv_ref.shape[0]):
        block = recv_ref[s].astype(f32)
        for k in range(SLOTS):
            held[s * SLOTS + k] = block[:, k * STATE : (k + 1) * STATE]
    for s in range(recv_ref.shape[0]):
        for j in range(REQS):
            picked_ref[s, :, j * STATE : (j + 1) * STATE] = held[hit_ref[s * REQS + j]].astype(bf16)
    copy = pltpu.make_async_copy(picked_ref, out_ref.at[:, :, 0 : REQS * STATE], sem)
    copy.start()
    copy.wait()


def make_snapshots(place_ref, after_ref, picked_ref, recv_ref, out_ref):
    del after_ref
    for s in range(recv_ref.shape[0]):
        prefix = picked_ref[s].astype(f32)
        block = recv_ref[s, :, REQS * STATE :].astype(f32)
        kept = block[:, REQS * STATE :]
        for j in range(REQS):
            columns = slice(j * STATE, (j + 1) * STATE)
            factor = kept[j : j + 1, :] + kept[REQS + j : REQS + j + 1, :]
            new = factor * prefix[:, columns] + block[:, columns]
            place = place_ref[s * REQS + j]
            start = pl.multiple_of((place & 3) * STATE, STATE)
            out_ref[place >> 2, :, pl.ds(start, STATE)] = new.astype(bf16)


def write_cache(missing_ref, cache_ref, recv_ref, out_ref):
    missing = missing_ref[0]
    for s in range(SLOTS):

        @pl.when(missing == s)
        def _():
            out_ref[s] = cache_ref[s]

        if s < REQS:

            @pl.when(missing > s)
            def _():
                out_ref[s] = recv_ref[:, s * STATE : (s + 1) * STATE].astype(f32)

        if s > 0:

            @pl.when(missing < s)
            def _():
                out_ref[s] = recv_ref[:, (s - 1) * STATE : s * STATE].astype(f32)


def token_inner(len_ref, me_ref, rate_ref, skip_ref, *refs):
    pair_refs, (base_ref, factor_ref, read_ref, tok_ref, gates, sems) = refs[:-6], refs[-6:]
    chips = len(pair_refs) // 2
    length = tok_ref.shape[0]
    heads = rate_ref.shape[1]
    width = heads * HEAD_DIM
    for copy in fetch(me_ref[0], pair_refs[:chips], tok_ref, sems.at[0]):
        copy.wait()
    copies = fetch(me_ref[0], pair_refs[chips:], gates, sems.at[1])
    ends = segment_ends(len_ref)
    step_size = jax.nn.softplus(tok_ref[:, width + STATE : width + STATE + heads].astype(f32))
    log_decay = -step_size * rate_ref[...]
    row = lax.broadcasted_iota(jnp.int32, (length, length), 0)
    column = lax.broadcasted_iota(jnp.int32, (length, length), 1)
    upto = (segment_of(row, ends) == segment_of(column, ends)) & (column <= row)
    running = exact_left(upto.astype(f32).astype(bf16), log_decay)
    spread = spread_heads(heads, width)
    decay = exact_right(jnp.exp(running), spread)
    undo = exact_right(jnp.exp(-running) * step_size, spread, 2)
    values = tok_ref[:, 0:width].astype(f32)
    b_half = tok_ref[:, width : width + STATE]
    for copy in copies:
        copy.wait()
    c_half = gates[:, width : width + STATE]
    c_wide = c_half.astype(f32)
    scores = jnp.where(upto, dot_nt(c_half, b_half), 0.0).astype(bf16)
    token = lax.broadcasted_iota(jnp.int32, (length, STATE), 0)
    seg_index = segment_of(token, ends)
    for j in range(REQS):
        read_ref[:, j * STATE : (j + 1) * STATE] = jnp.where(seg_index == j, c_wide, 0.0).astype(
            bf16
        )
    inner = dot(scores, (undo * values).astype(bf16))
    gate_in = gates[:, 0:width].astype(f32)
    gate = gate_in / (1.0 + jnp.exp(-gate_in))
    base_ref[...] = gate * (decay * inner + exact_right(skip_ref[...], spread) * values)
    factor_ref[...] = gate * decay


def token_outputs(gain_ref, base_ref, factor_ref, read_ref, recv_ref, out_ref):
    carried = dot_nt(read_ref[...], recv_ref[:, 0 : REQS * STATE])
    gated = base_ref[...] + factor_ref[...] * carried
    square_mean = jnp.mean(gated * gated, axis=1, keepdims=True)
    out_ref[...] = (gated * lax.rsqrt(square_mean + 1e-05) * gain_ref[...]).astype(bf16)


def gated_norm(values, gate_in, norm_weight):
    shaped = values.shape
    gated = values * jax.nn.silu(gate_in.astype(jnp.float32).reshape(shaped))
    square_mean = jnp.mean(gated * gated, axis=(2, 3), keepdims=True)
    normed = gated * lax.rsqrt(square_mean + 1e-05) * norm_weight.reshape(shaped[1:])
    return normed.reshape(shaped[0], -1).astype(jnp.bfloat16)


def decode_block(
    inputs, gate_in, b_proj, c_proj, step_raw, states, head_rates, skip_gain, norm_weight
):
    row_count = inputs.shape[0]
    head_count = step_raw.shape[1]
    groups = b_proj.shape[1] // STATE
    per_group = head_count // groups
    step_size = jax.nn.softplus(step_raw.astype(jnp.float32))
    factor = jnp.exp(-step_size * head_rates[None, :]).reshape(row_count, groups, per_group, 1, 1)
    values = inputs.astype(jnp.float32).reshape(row_count, groups, per_group, HEAD_DIM)
    b_group = b_proj.astype(jnp.float32).reshape(row_count, groups, STATE)
    c_group = c_proj.astype(jnp.float32).reshape(row_count, groups, STATE)
    written = (step_size.reshape(row_count, groups, per_group, 1) * values)[..., None] * b_group[
        :, :, None, None, :
    ]
    updated = factor * states.reshape(row_count, groups, per_group, HEAD_DIM, STATE) + written
    outputs = (
        jnp.einsum("rgkpn,rgn->rgkp", updated, c_group, precision=highest)
        + skip_gain.reshape(groups, per_group, 1) * values
    )
    return (
        gated_norm(outputs, gate_in, norm_weight),
        updated.reshape(row_count, head_count, HEAD_DIM, STATE),
    )


def local(
    pre_x,
    pre_z,
    pre_b,
    pre_c,
    pre_dt,
    suffix_lengths,
    prefix_hits,
    snapshot_slots,
    cache_states,
    dec_x,
    dec_z,
    dec_b,
    dec_c,
    dec_dt,
    dec_states,
    decay_rate,
    d_skip,
    norm_weight,
):
    n_head = lax.axis_size("head")
    n_serve = lax.axis_size("serve")
    rows = pre_x.shape[0]
    heads = cache_states.shape[1]
    width = heads * HEAD_DIM
    length = rows * n_head
    tiles = 2 * REQS + 1
    shape = jax.ShapeDtypeStruct

    def swap(value):
        return lax.all_to_all(value, "serve", split_axis=0, concat_axis=0, tiled=True)

    chips = n_head // 2
    with jax.named_scope("orders"):
        head_me = lax.axis_index("head").astype(jnp.int32).reshape(1)
        rank = jnp.sum(
            (snapshot_slots[None, :] < snapshot_slots[:, None]).astype(jnp.int32), axis=1
        )
        place = (rank // REQS) * 4 + rank % REQS
        serve_me = lax.axis_index("serve")
        missing = (
            sum(range(SLOTS))
            - jnp.sum(jnp.where(snapshot_slots // SLOTS == serve_me, snapshot_slots % SLOTS, 0))
        ).reshape(1)
    with jax.named_scope("cache"):
        cache_rows = cache_states.reshape(SLOTS, width, STATE)
        spread = pl.pallas_call(
            pack_cache,
            out_shape=shape((width, SLOTS * STATE), bf16),
            in_specs=[VMEM],
            out_specs=VMEM,
            compiler_params=params(),
            cost_estimate=cost(0, 1_600_000),
        )(cache_rows)
        pieces = swap(spread.reshape(n_serve, ROWS, SLOTS * STATE))
    with jax.named_scope("tokens"):
        keep, give = pl.pallas_call(
            pack_tokens,
            out_shape=[shape((chips, rows, width + 2 * STATE), bf16)] * 2,
            in_specs=[SMEM, ANY] + [VMEM] * 3,
            out_specs=[VMEM] * 2,
            compiler_params=params(),
            cost_estimate=cost(0, 800_000),
        )(head_me, spread, pre_x, pre_b, pre_dt)
        tokens = exchange(keep, give, n_head)
    rates = decay_rate.reshape(1, heads)
    with jax.named_scope("prefix"):
        send, picked = pl.pallas_call(
            pick_prefix,
            out_shape=(
                shape((n_serve, ROWS, tiles * STATE), bf16),
                shape((n_serve, ROWS, REQS * STATE), bf16),
            ),
            in_specs=[SMEM, VMEM],
            out_specs=(HBM, VMEM),
            scratch_shapes=[
                pltpu.VMEM((n_serve * SLOTS, ROWS, STATE), f32),
                pltpu.SemaphoreType.DMA,
            ],
            compiler_params=params(),
            cost_estimate=cost(0, 2_000_000),
        )(prefix_hits, pieces)
    with jax.named_scope("local"):
        send = pl.pallas_call(
            local_state,
            out_shape=shape((width, tiles * STATE), bf16),
            in_specs=[SMEM] * 2 + [VMEM] + [ANY] * chips + [HBM],
            out_specs=HBM,
            scratch_shapes=[
                pltpu.VMEM((length, width + 2 * STATE), bf16),
                pltpu.VMEM((width, (REQS + 1) * STATE), bf16),
                pltpu.SemaphoreType.DMA((n_head,)),
                pltpu.SemaphoreType.DMA,
            ],
            input_output_aliases={3 + chips: 0},
            compiler_params=params(),
            cost_estimate=cost(300_000_000, 800_000),
        )(suffix_lengths, head_me, rates, *tokens, send.reshape(width, tiles * STATE))
        got = swap(send.reshape(n_serve, ROWS, tiles * STATE))
    with jax.named_scope("gates"):
        keep, give = pl.pallas_call(
            pack_gates,
            out_shape=[shape((chips, rows, width + STATE), bf16)] * 2,
            in_specs=[SMEM, ANY] + [VMEM] * 2,
            out_specs=[VMEM] * 2,
            compiler_params=params(),
            cost_estimate=cost(0, 650_000),
        )(head_me, send, pre_z, pre_c)
        gates = exchange(keep, give, n_head)
    with jax.named_scope("inner"):
        base, factor, read = pl.pallas_call(
            token_inner,
            out_shape=(
                shape((length, width), f32),
                shape((length, width), f32),
                shape((length, REQS * STATE), bf16),
            ),
            in_specs=[SMEM] * 2 + [VMEM] * 2 + [ANY] * n_head,
            out_specs=[VMEM] * 3,
            scratch_shapes=[
                pltpu.VMEM((length, width + 2 * STATE), bf16),
                pltpu.VMEM((length, width + STATE), bf16),
                pltpu.SemaphoreType.DMA((2, n_head)),
            ],
            compiler_params=params(),
            cost_estimate=cost(400_000_000, 1_500_000),
        )(suffix_lengths, head_me, rates, d_skip.reshape(1, heads), *tokens, *gates)
    with jax.named_scope("snapshots"):
        answer = pl.pallas_call(
            make_snapshots,
            out_shape=shape((n_serve, ROWS, REQS * STATE), bf16),
            in_specs=[SMEM, ANY, VMEM, VMEM],
            out_specs=VMEM,
            compiler_params=params(),
            cost_estimate=cost(0, 2_000_000),
        )(place, read, picked, got)
        new = swap(answer).reshape(width, REQS * STATE)
    dec_out, dec_new = decode_block(
        dec_x, dec_z, dec_b, dec_c, dec_dt, dec_states, decay_rate, d_skip, norm_weight
    )
    with jax.named_scope("outputs"):
        pre_out = pl.pallas_call(
            token_outputs,
            out_shape=shape((length, width), bf16),
            in_specs=[VMEM] * 5,
            out_specs=VMEM,
            compiler_params=params(),
            cost_estimate=cost(200_000_000, 1_500_000),
        )(norm_weight.reshape(1, width), base, factor, read, got.reshape(width, tiles * STATE))
        cache_out = pl.pallas_call(
            write_cache,
            out_shape=shape((SLOTS, width, STATE), f32),
            in_specs=[SMEM, VMEM, VMEM],
            out_specs=VMEM,
            compiler_params=params(),
            cost_estimate=cost(0, 2_500_000),
        )(missing, cache_rows, new).reshape(cache_states.shape)
    return (pre_out, cache_out, dec_out, dec_new)


def solution(mesh):
    return jax.shard_map(
        local,
        mesh=mesh,
        in_specs=(
            P(("serve", "head"), None),
            P(("serve", "head"), None),
            P(("serve", "head"), None),
            P(("serve", "head"), None),
            P(("serve", "head"), None),
            P("serve", None),
            P(),
            P(),
            P("serve", "head", None, None),
            P("serve", "head"),
            P("serve", "head"),
            P("serve", "head"),
            P("serve", "head"),
            P("serve", "head"),
            P("serve", "head", None, None),
            P("head"),
            P("head"),
            P("head"),
        ),
        out_specs=(
            P("serve", "head"),
            P("serve", "head", None, None),
            P("serve", "head"),
            P("serve", "head", None, None),
        ),
        check_vma=False,
    )
```

```python
import jax
import jax.numpy as jnp
from jax import lax
from jax.experimental import pallas as pl
from jax.experimental.pallas import tpu as pltpu
from jax.sharding import PartitionSpec as P

HEAD_DIM = 64
STATE = 128
REQS = 3
SLOTS = 4
ROWS = 8

f32 = jnp.float32
bf16 = jnp.bfloat16
highest = lax.Precision.HIGHEST

ANY = pl.BlockSpec(memory_space=pl.ANY)
HBM = pl.BlockSpec(memory_space=pltpu.HBM)
VMEM = pl.BlockSpec(memory_space=pltpu.VMEM)
SMEM = pl.BlockSpec(memory_space=pltpu.SMEM)


def params(mib=12):
    return pltpu.CompilerParams(vmem_limit_bytes=mib * 1024 * 1024)


def cost(flops, moved):
    return pl.CostEstimate(flops=flops, bytes_accessed=moved, transcendentals=0)


def dot(a, b):
    return jnp.dot(a, b, preferred_element_type=f32)


def dot_nt(a, b):
    return lax.dot_general(a, b, (((1,), (1,)), ((), ())), preferred_element_type=f32)


def dot_tn(a, b):
    return lax.dot_general(a, b, (((0,), (0,)), ((), ())), preferred_element_type=f32)


def split(value, parts):
    pieces = []
    for _ in range(parts):
        piece = value.astype(bf16)
        pieces.append(piece)
        value = value - piece.astype(f32)
    return pieces


def exact_left(mask, value, parts=3):
    total = None
    for piece in split(value, parts):
        term = dot(mask, piece)
        total = term if total is None else total + term
    return total


def exact_right(value, mask, parts=3):
    total = None
    for piece in split(value, parts):
        term = dot(piece, mask)
        total = term if total is None else total + term
    return total


def pack_tokens(me_ref, after_ref, x_ref, b_ref, dt_ref, keep_ref, give_ref):
    del after_ref
    chips = keep_ref.shape[0]
    heads_dev = dt_ref.shape[1] // (2 * chips)
    width = x_ref.shape[1] // (2 * chips)
    raw = dt_ref[...].astype(f32)
    raw = jnp.concatenate([raw, jnp.zeros((raw.shape[0], STATE - raw.shape[1]), f32)], axis=1)
    for side, ref in enumerate((keep_ref, give_ref)):
        for k in range(chips):
            peer = me_ref[0] ^ (2 * k + side)
            x_start = pl.multiple_of(peer * width, STATE)
            b_start = pl.multiple_of(peer * STATE, STATE)
            ref[k, :, 0:width] = x_ref[:, pl.ds(x_start, width)]
            ref[k, :, width : width + STATE] = b_ref[:, pl.ds(b_start, STATE)]
            mine = pltpu.roll(raw, (STATE - peer * heads_dev) % STATE, 1)
            ref[k, :, width + STATE : width + 2 * STATE] = mine.astype(bf16)


def pack_gates(me_ref, after_ref, z_ref, c_ref, keep_ref, give_ref):
    del after_ref
    chips = keep_ref.shape[0]
    width = z_ref.shape[1] // (2 * chips)
    for side, ref in enumerate((keep_ref, give_ref)):
        for k in range(chips):
            peer = me_ref[0] ^ (2 * k + side)
            z_start = pl.multiple_of(peer * width, STATE)
            c_start = pl.multiple_of(peer * STATE, STATE)
            ref[k, :, 0:width] = z_ref[:, pl.ds(z_start, width)]
            ref[k, :, width : width + STATE] = c_ref[:, pl.ds(c_start, STATE)]


def pair_up(keep_ref, got_ref, *out_refs):
    for k, ref in enumerate(out_refs):
        ref[0] = keep_ref[k]
        ref[1] = got_ref[k]


def exchange(keep, give, n_head):
    chips = n_head // 2
    shape = jax.ShapeDtypeStruct((2,) + keep.shape[1:], bf16)
    got = lax.ppermute(give, "head", [(i, i ^ 1) for i in range(n_head)])
    pairs = pl.pallas_call(
        pair_up,
        out_shape=[shape] * chips,
        in_specs=[VMEM] * 2,
        out_specs=[VMEM] * chips,
        compiler_params=params(),
        cost_estimate=cost(0, 800_000),
    )(keep, got)
    return [pairs[0]] + [
        lax.ppermute(pairs[k], "head", [(i, i ^ (2 * k)) for i in range(n_head)])
        for k in range(1, chips)
    ]


def fetch(me, pair_refs, rows_ref, sems):
    rows = pair_refs[0].shape[1]
    copies = []
    for k, ref in enumerate(pair_refs):
        for side in range(2):
            start = pl.multiple_of((me ^ (2 * k + side)) * rows, rows)
            copies.append(
                pltpu.make_async_copy(
                    ref.at[side], rows_ref.at[pl.ds(start, rows), :], sems.at[2 * k + side]
                )
            )
    for copy in copies:
        copy.start()
    return copies


def pack_cache(cache_ref, out_ref):
    for s in range(SLOTS):
        out_ref[:, s * STATE : (s + 1) * STATE] = cache_ref[s].astype(bf16)


def segment_of(position, ends):
    return (position >= ends[0]).astype(jnp.int32) + (position >= ends[1]).astype(jnp.int32)


def segment_ends(len_ref):
    first = len_ref[0, 0]
    return first, first + len_ref[0, 1]


def spread_heads(heads, width):
    row = lax.broadcasted_iota(jnp.int32, (heads, width), 0)
    column = lax.broadcasted_iota(jnp.int32, (heads, width), 1)
    return (row == column // (width // heads)).astype(bf16)


def local_state(len_ref, me_ref, rate_ref, *refs):
    pair_refs, (out_ref, tok_ref, made, sems, last_sem) = refs[:-5], refs[-5:]
    length = tok_ref.shape[0]
    heads = rate_ref.shape[1]
    width = heads * HEAD_DIM
    for copy in fetch(me_ref[0], pair_refs, tok_ref, sems):
        copy.wait()
    ends = segment_ends(len_ref)
    step_size = jax.nn.softplus(tok_ref[:, width + STATE : width + STATE + heads].astype(f32))
    log_decay = -step_size * rate_ref[...]
    row = lax.broadcasted_iota(jnp.int32, (length, length), 0)
    column = lax.broadcasted_iota(jnp.int32, (length, length), 1)
    later = (segment_of(row, ends) == segment_of(column, ends)) & (column > row)
    after = exact_left(later.astype(f32).astype(bf16), log_decay)
    weight = exact_right(jnp.exp(after) * step_size, spread_heads(heads, width), 2)
    scaled = (weight * tok_ref[:, 0:width].astype(f32)).astype(bf16)
    token = lax.broadcasted_iota(jnp.int32, (length, STATE), 0)
    lane = lax.broadcasted_iota(jnp.int32, (length, STATE), 1)
    seg_index = segment_of(token, ends)
    b_half = tok_ref[:, width : width + STATE].astype(f32)
    b_parts = jnp.concatenate(
        [jnp.where(seg_index == j, b_half, 0.0).astype(bf16) for j in range(REQS)], axis=1
    )
    made[:, 0 : REQS * STATE] = dot_tn(scaled, b_parts).astype(bf16)
    member = (seg_index == lane % REQS).astype(f32).astype(bf16)
    total = None
    for piece in split(log_decay, 3):
        term = dot_tn(piece, member)
        total = term if total is None else total + term
    kept = jnp.exp(total)
    high = kept.astype(bf16).astype(f32)
    lane_h = lax.broadcasted_iota(jnp.int32, (heads, STATE), 1)
    parts = jnp.where(lane_h < REQS, high, jnp.where(lane_h < 2 * REQS, kept - high, 0.0))
    row_w = lax.broadcasted_iota(jnp.int32, (width, heads), 0)
    col_w = lax.broadcasted_iota(jnp.int32, (width, heads), 1)
    owner = (row_w // HEAD_DIM == col_w).astype(f32).astype(bf16)
    spread = dot(owner, parts.astype(bf16))
    row_s = lax.broadcasted_iota(jnp.int32, (width, STATE), 0)
    lane_s = lax.broadcasted_iota(jnp.int32, (width, STATE), 1)
    chosen = jnp.where(lane_s == row_s % ROWS, spread, 0.0).astype(bf16)
    made[:, REQS * STATE :] = dot(chosen, jnp.ones((STATE, STATE), bf16)).astype(bf16)
    last = pltpu.make_async_copy(made, out_ref.at[:, REQS * STATE :], last_sem)
    last.start()
    last.wait()


def pick_prefix(hit_ref, recv_ref, send_ref, out_ref, picked_ref, held, sem):
    del send_ref
    for s in range(recv_ref.shape[0]):
        block = recv_ref[s].astype(f32)
        for k in range(SLOTS):
            held[s * SLOTS + k] = block[:, k * STATE : (k + 1) * STATE]
    for s in range(recv_ref.shape[0]):
        for j in range(REQS):
            picked_ref[s, :, j * STATE : (j + 1) * STATE] = held[hit_ref[s * REQS + j]].astype(bf16)
    copy = pltpu.make_async_copy(picked_ref, out_ref.at[:, :, 0 : REQS * STATE], sem)
    copy.start()
    copy.wait()


def make_snapshots(place_ref, picked_ref, recv_ref, *refs):
    out_ref = refs[-1]
    for s in range(recv_ref.shape[0]):
        prefix = picked_ref[s].astype(f32)
        block = recv_ref[s, :, REQS * STATE :].astype(f32)
        kept = block[:, REQS * STATE :]
        for j in range(REQS):
            columns = slice(j * STATE, (j + 1) * STATE)
            factor = kept[j : j + 1, :] + kept[REQS + j : REQS + j + 1, :]
            new = factor * prefix[:, columns] + block[:, columns]
            place = place_ref[s * REQS + j]
            start = pl.multiple_of((place & 3) * STATE, STATE)
            out_ref[place >> 2, :, pl.ds(start, STATE)] = new.astype(bf16)


def write_cache(missing_ref, cache_ref, recv_ref, out_ref):
    missing = missing_ref[0]
    for s in range(SLOTS):

        @pl.when(missing == s)
        def _():
            out_ref[s] = cache_ref[s]

        if s < REQS:

            @pl.when(missing > s)
            def _():
                out_ref[s] = recv_ref[:, s * STATE : (s + 1) * STATE].astype(f32)

        if s > 0:

            @pl.when(missing < s)
            def _():
                out_ref[s] = recv_ref[:, (s - 1) * STATE : s * STATE].astype(f32)


def token_inner(len_ref, me_ref, rate_ref, skip_ref, *refs):
    pair_refs, (base_ref, factor_ref, read_ref, tok_ref, gates, sems) = refs[:-6], refs[-6:]
    chips = len(pair_refs) // 2
    length = tok_ref.shape[0]
    heads = rate_ref.shape[1]
    width = heads * HEAD_DIM
    for copy in fetch(me_ref[0], pair_refs[:chips], tok_ref, sems.at[0]):
        copy.wait()
    copies = fetch(me_ref[0], pair_refs[chips:], gates, sems.at[1])
    ends = segment_ends(len_ref)
    step_size = jax.nn.softplus(tok_ref[:, width + STATE : width + STATE + heads].astype(f32))
    log_decay = -step_size * rate_ref[...]
    row = lax.broadcasted_iota(jnp.int32, (length, length), 0)
    column = lax.broadcasted_iota(jnp.int32, (length, length), 1)
    upto = (segment_of(row, ends) == segment_of(column, ends)) & (column <= row)
    running = exact_left(upto.astype(f32).astype(bf16), log_decay)
    spread = spread_heads(heads, width)
    decay = exact_right(jnp.exp(running), spread)
    undo = exact_right(jnp.exp(-running) * step_size, spread, 2)
    values = tok_ref[:, 0:width].astype(f32)
    b_half = tok_ref[:, width : width + STATE]
    for copy in copies:
        copy.wait()
    c_half = gates[:, width : width + STATE]
    c_wide = c_half.astype(f32)
    scores = jnp.where(upto, dot_nt(c_half, b_half), 0.0).astype(bf16)
    token = lax.broadcasted_iota(jnp.int32, (length, STATE), 0)
    seg_index = segment_of(token, ends)
    for j in range(REQS):
        read_ref[:, j * STATE : (j + 1) * STATE] = jnp.where(seg_index == j, c_wide, 0.0).astype(
            bf16
        )
    inner = dot(scores, (undo * values).astype(bf16))
    gate_in = gates[:, 0:width].astype(f32)
    gate = gate_in / (1.0 + jnp.exp(-gate_in))
    base_ref[...] = gate * (decay * inner + exact_right(skip_ref[...], spread) * values)
    factor_ref[...] = gate * decay


def token_outputs(gain_ref, base_ref, factor_ref, read_ref, recv_ref, out_ref):
    carried = dot_nt(read_ref[...], recv_ref[:, 0 : REQS * STATE])
    gated = base_ref[...] + factor_ref[...] * carried
    square_mean = jnp.mean(gated * gated, axis=1, keepdims=True)
    out_ref[...] = (gated * lax.rsqrt(square_mean + 1e-05) * gain_ref[...]).astype(bf16)


def gated_norm(values, gate_in, norm_weight):
    shaped = values.shape
    gated = values * jax.nn.silu(gate_in.astype(jnp.float32).reshape(shaped))
    square_mean = jnp.mean(gated * gated, axis=(2, 3), keepdims=True)
    normed = gated * lax.rsqrt(square_mean + 1e-05) * norm_weight.reshape(shaped[1:])
    return normed.reshape(shaped[0], -1).astype(jnp.bfloat16)


def decode_block(
    inputs, gate_in, b_proj, c_proj, step_raw, states, head_rates, skip_gain, norm_weight
):
    row_count = inputs.shape[0]
    head_count = step_raw.shape[1]
    groups = b_proj.shape[1] // STATE
    per_group = head_count // groups
    step_size = jax.nn.softplus(step_raw.astype(jnp.float32))
    factor = jnp.exp(-step_size * head_rates[None, :]).reshape(row_count, groups, per_group, 1, 1)
    values = inputs.astype(jnp.float32).reshape(row_count, groups, per_group, HEAD_DIM)
    b_group = b_proj.astype(jnp.float32).reshape(row_count, groups, STATE)
    c_group = c_proj.astype(jnp.float32).reshape(row_count, groups, STATE)
    written = (step_size.reshape(row_count, groups, per_group, 1) * values)[..., None] * b_group[
        :, :, None, None, :
    ]
    updated = factor * states.reshape(row_count, groups, per_group, HEAD_DIM, STATE) + written
    outputs = (
        jnp.einsum("rgkpn,rgn->rgkp", updated, c_group, precision=highest)
        + skip_gain.reshape(groups, per_group, 1) * values
    )
    return (
        gated_norm(outputs, gate_in, norm_weight),
        updated.reshape(row_count, head_count, HEAD_DIM, STATE),
    )


def local(
    pre_x,
    pre_z,
    pre_b,
    pre_c,
    pre_dt,
    suffix_lengths,
    prefix_hits,
    snapshot_slots,
    cache_states,
    dec_x,
    dec_z,
    dec_b,
    dec_c,
    dec_dt,
    dec_states,
    decay_rate,
    d_skip,
    norm_weight,
):
    n_head = lax.axis_size("head")
    n_serve = lax.axis_size("serve")
    rows = pre_x.shape[0]
    heads = cache_states.shape[1]
    width = heads * HEAD_DIM
    length = rows * n_head
    tiles = 2 * REQS + 1
    shape = jax.ShapeDtypeStruct

    def swap(value):
        return lax.all_to_all(value, "serve", split_axis=0, concat_axis=0, tiled=True)

    chips = n_head // 2
    with jax.named_scope("orders"):
        head_me = lax.axis_index("head").astype(jnp.int32).reshape(1)
        rank = jnp.sum(
            (snapshot_slots[None, :] < snapshot_slots[:, None]).astype(jnp.int32), axis=1
        )
        place = (rank // REQS) * 4 + rank % REQS
        serve_me = lax.axis_index("serve")
        missing = (
            sum(range(SLOTS))
            - jnp.sum(jnp.where(snapshot_slots // SLOTS == serve_me, snapshot_slots % SLOTS, 0))
        ).reshape(1)
    with jax.named_scope("cache"):
        cache_rows = cache_states.reshape(SLOTS, width, STATE)
        spread = pl.pallas_call(
            pack_cache,
            out_shape=shape((width, SLOTS * STATE), bf16),
            in_specs=[VMEM],
            out_specs=VMEM,
            compiler_params=params(),
            cost_estimate=cost(0, 1_600_000),
        )(cache_rows)
        pieces = swap(spread.reshape(n_serve, ROWS, SLOTS * STATE))
    with jax.named_scope("tokens"):
        keep, give = pl.pallas_call(
            pack_tokens,
            out_shape=[shape((chips, rows, width + 2 * STATE), bf16)] * 2,
            in_specs=[SMEM, ANY] + [VMEM] * 3,
            out_specs=[VMEM] * 2,
            compiler_params=params(),
            cost_estimate=cost(0, 800_000),
        )(head_me, spread, pre_x, pre_b, pre_dt)
        tokens = exchange(keep, give, n_head)
    rates = decay_rate.reshape(1, heads)
    with jax.named_scope("local"):
        send = pl.pallas_call(
            local_state,
            out_shape=shape((width, tiles * STATE), bf16),
            in_specs=[SMEM] * 2 + [VMEM] + [ANY] * chips,
            out_specs=HBM,
            scratch_shapes=[
                pltpu.VMEM((length, width + 2 * STATE), bf16),
                pltpu.VMEM((width, (REQS + 1) * STATE), bf16),
                pltpu.SemaphoreType.DMA((n_head,)),
                pltpu.SemaphoreType.DMA,
            ],
            compiler_params=params(),
            cost_estimate=cost(300_000_000, 800_000),
        )(suffix_lengths, head_me, rates, *tokens)
    with jax.named_scope("prefix"):
        send, picked = pl.pallas_call(
            pick_prefix,
            out_shape=(
                shape((n_serve, ROWS, tiles * STATE), bf16),
                shape((n_serve, ROWS, REQS * STATE), bf16),
            ),
            in_specs=[SMEM, VMEM, HBM],
            out_specs=(HBM, VMEM),
            scratch_shapes=[
                pltpu.VMEM((n_serve * SLOTS, ROWS, STATE), f32),
                pltpu.SemaphoreType.DMA,
            ],
            input_output_aliases={2: 0},
            compiler_params=params(),
            cost_estimate=cost(0, 2_000_000),
        )(prefix_hits, pieces, send.reshape(n_serve, ROWS, tiles * STATE))
        got = swap(send)
    with jax.named_scope("gates"):
        keep, give = pl.pallas_call(
            pack_gates,
            out_shape=[shape((chips, rows, width + STATE), bf16)] * 2,
            in_specs=[SMEM, ANY] + [VMEM] * 2,
            out_specs=[VMEM] * 2,
            compiler_params=params(),
            cost_estimate=cost(0, 650_000),
        )(head_me, send, pre_z, pre_c)
        gates = exchange(keep, give, n_head)
    with jax.named_scope("inner"):
        base, factor, read = pl.pallas_call(
            token_inner,
            out_shape=(
                shape((length, width), f32),
                shape((length, width), f32),
                shape((length, REQS * STATE), bf16),
            ),
            in_specs=[SMEM] * 2 + [VMEM] * 2 + [ANY] * n_head,
            out_specs=[VMEM] * 3,
            scratch_shapes=[
                pltpu.VMEM((length, width + 2 * STATE), bf16),
                pltpu.VMEM((length, width + STATE), bf16),
                pltpu.SemaphoreType.DMA((2, n_head)),
            ],
            compiler_params=params(),
            cost_estimate=cost(400_000_000, 1_500_000),
        )(suffix_lengths, head_me, rates, d_skip.reshape(1, heads), *tokens, *gates)
    with jax.named_scope("snapshots"):
        answer = pl.pallas_call(
            make_snapshots,
            out_shape=shape((n_serve, ROWS, REQS * STATE), bf16),
            in_specs=[SMEM, VMEM, VMEM] + [ANY] * (chips - 1),
            out_specs=VMEM,
            compiler_params=params(),
            cost_estimate=cost(0, 2_000_000),
        )(place, picked, got, *gates[1:])
        new = swap(answer).reshape(width, REQS * STATE)
    dec_out, dec_new = decode_block(
        dec_x, dec_z, dec_b, dec_c, dec_dt, dec_states, decay_rate, d_skip, norm_weight
    )
    with jax.named_scope("outputs"):
        pre_out = pl.pallas_call(
            token_outputs,
            out_shape=shape((length, width), bf16),
            in_specs=[VMEM] * 5,
            out_specs=VMEM,
            compiler_params=params(),
            cost_estimate=cost(200_000_000, 1_500_000),
        )(norm_weight.reshape(1, width), base, factor, read, got.reshape(width, tiles * STATE))
        cache_out = pl.pallas_call(
            write_cache,
            out_shape=shape((SLOTS, width, STATE), f32),
            in_specs=[SMEM, VMEM, VMEM],
            out_specs=VMEM,
            compiler_params=params(),
            cost_estimate=cost(0, 2_500_000),
        )(missing, cache_rows, new).reshape(cache_states.shape)
    return (pre_out, cache_out, dec_out, dec_new)


def solution(mesh):
    return jax.shard_map(
        local,
        mesh=mesh,
        in_specs=(
            P(("serve", "head"), None),
            P(("serve", "head"), None),
            P(("serve", "head"), None),
            P(("serve", "head"), None),
            P(("serve", "head"), None),
            P("serve", None),
            P(),
            P(),
            P("serve", "head", None, None),
            P("serve", "head"),
            P("serve", "head"),
            P("serve", "head"),
            P("serve", "head"),
            P("serve", "head"),
            P("serve", "head", None, None),
            P("head"),
            P("head"),
            P("head"),
        ),
        out_specs=(
            P("serve", "head"),
            P("serve", "head", None, None),
            P("serve", "head"),
            P("serve", "head", None, None),
        ),
        check_vma=False,
    )
```

```python
import jax
import jax.numpy as jnp
from jax import lax
from jax.experimental import pallas as pl
from jax.experimental.pallas import tpu as pltpu
from jax.sharding import PartitionSpec as P

HEAD_DIM = 64
STATE = 128
REQS = 3
SLOTS = 4
ROWS = 8

f32 = jnp.float32
bf16 = jnp.bfloat16
highest = lax.Precision.HIGHEST

ANY = pl.BlockSpec(memory_space=pl.ANY)
HBM = pl.BlockSpec(memory_space=pltpu.HBM)
VMEM = pl.BlockSpec(memory_space=pltpu.VMEM)
SMEM = pl.BlockSpec(memory_space=pltpu.SMEM)


def params(mib=12):
    return pltpu.CompilerParams(vmem_limit_bytes=mib * 1024 * 1024)


def cost(flops, moved):
    return pl.CostEstimate(flops=flops, bytes_accessed=moved, transcendentals=0)


def dot(a, b):
    return jnp.dot(a, b, preferred_element_type=f32)


def dot_nt(a, b):
    return lax.dot_general(a, b, (((1,), (1,)), ((), ())), preferred_element_type=f32)


def dot_tn(a, b):
    return lax.dot_general(a, b, (((0,), (0,)), ((), ())), preferred_element_type=f32)


def split(value, parts):
    pieces = []
    for _ in range(parts):
        piece = value.astype(bf16)
        pieces.append(piece)
        value = value - piece.astype(f32)
    return pieces


def exact_left(mask, value, parts=3):
    total = None
    for piece in split(value, parts):
        term = dot(mask, piece)
        total = term if total is None else total + term
    return total


def exact_right(value, mask, parts=3):
    total = None
    for piece in split(value, parts):
        term = dot(piece, mask)
        total = term if total is None else total + term
    return total


def pack_first(
    x_ref, b_ref, dt_ref, rate_ref, len_ref, out_ref, meta_ref, xs, bs, steps, rates, lens, sems
):
    count = out_ref.shape[0]
    heads_dev = dt_ref.shape[1] // count
    width = x_ref.shape[1] // count
    copies = [
        pltpu.make_async_copy(src, dst, sems.at[i])
        for i, (src, dst) in enumerate(
            ((x_ref, xs), (b_ref, bs), (dt_ref, steps), (rate_ref, rates), (len_ref, lens))
        )
    ]
    for copy in copies:
        copy.start()
    for copy in copies:
        copy.wait()
    raw = steps[...].astype(f32)
    raw = jnp.concatenate([raw, jnp.zeros((raw.shape[0], STATE - raw.shape[1]), f32)], axis=1)
    for d in range(count):
        out_ref[d, :, 0:width] = xs[:, d * width : (d + 1) * width]
        out_ref[d, :, width : width + STATE] = bs[:, d * STATE : (d + 1) * STATE]
        mine = raw if d == 0 else pltpu.roll(raw, STATE - d * heads_dev, 1)
        out_ref[d, :, width + STATE : width + 2 * STATE] = mine.astype(bf16)
    meta_ref[...] = jnp.zeros_like(meta_ref)
    meta_ref[0:1, 0 : rates.shape[1]] = rates[...]
    meta_ref[1:2, 0:1] = lens[:, 0:1].astype(f32)
    meta_ref[2:3, 0:1] = (lens[:, 0:1] + lens[:, 1:2]).astype(f32)


def pack_gates(me_ref, after_ref, z_ref, c_ref, keep_ref, give_ref):
    del after_ref
    chips = keep_ref.shape[0]
    width = z_ref.shape[1] // (2 * chips)
    for side, ref in enumerate((keep_ref, give_ref)):
        for k in range(chips):
            peer = me_ref[0] ^ (2 * k + side)
            z_start = pl.multiple_of(peer * width, STATE)
            c_start = pl.multiple_of(peer * STATE, STATE)
            ref[k, :, 0:width] = z_ref[:, pl.ds(z_start, width)]
            ref[k, :, width : width + STATE] = c_ref[:, pl.ds(c_start, STATE)]


def pair_up(keep_ref, got_ref, *out_refs):
    for k, ref in enumerate(out_refs):
        ref[0] = keep_ref[k]
        ref[1] = got_ref[k]


def exchange(keep, give, n_head):
    chips = n_head // 2
    shape = jax.ShapeDtypeStruct((2,) + keep.shape[1:], bf16)
    got = lax.ppermute(give, "head", [(i, i ^ 1) for i in range(n_head)])
    pairs = pl.pallas_call(
        pair_up,
        out_shape=[shape] * chips,
        in_specs=[VMEM] * 2,
        out_specs=[VMEM] * chips,
        compiler_params=params(),
        cost_estimate=cost(0, 800_000),
    )(keep, got)
    return [pairs[0]] + [
        lax.ppermute(pairs[k], "head", [(i, i ^ (2 * k)) for i in range(n_head)])
        for k in range(1, chips)
    ]


def fetch(me, pair_refs, rows_ref, sems):
    rows = pair_refs[0].shape[1]
    copies = []
    for k, ref in enumerate(pair_refs):
        for side in range(2):
            start = pl.multiple_of((me ^ (2 * k + side)) * rows, rows)
            copies.append(
                pltpu.make_async_copy(
                    ref.at[side], rows_ref.at[pl.ds(start, rows), :], sems.at[2 * k + side]
                )
            )
    for copy in copies:
        copy.start()
    return copies


def pack_cache(cache_ref, out_ref):
    for s in range(SLOTS):
        out_ref[:, s * STATE : (s + 1) * STATE] = cache_ref[s].astype(bf16)


def segment_of(position, ends):
    return (position >= ends[0]).astype(jnp.int32) + (position >= ends[1]).astype(jnp.int32)


def segment_ends(meta_ref):
    return meta_ref[1:2, 0:1].astype(jnp.int32), meta_ref[2:3, 0:1].astype(jnp.int32)


def spread_heads(heads, width):
    row = lax.broadcasted_iota(jnp.int32, (heads, width), 0)
    column = lax.broadcasted_iota(jnp.int32, (heads, width), 1)
    return (row == column // (width // heads)).astype(bf16)


def local_state(meta_ref, tok_ref, send_ref, out_ref):
    del send_ref
    length = tok_ref.shape[0]
    width = out_ref.shape[0]
    heads = width // HEAD_DIM
    ends = segment_ends(meta_ref)
    step_size = jax.nn.softplus(tok_ref[:, width + STATE : width + STATE + heads].astype(f32))
    log_decay = -step_size * meta_ref[0:1, 0:heads]
    row = lax.broadcasted_iota(jnp.int32, (length, length), 0)
    column = lax.broadcasted_iota(jnp.int32, (length, length), 1)
    later = (segment_of(row, ends) == segment_of(column, ends)) & (column > row)
    after = exact_left(later.astype(f32).astype(bf16), log_decay)
    weight = exact_right(jnp.exp(after) * step_size, spread_heads(heads, width), 2)
    scaled = (weight * tok_ref[:, 0:width].astype(f32)).astype(bf16)
    token = lax.broadcasted_iota(jnp.int32, (length, STATE), 0)
    lane = lax.broadcasted_iota(jnp.int32, (length, STATE), 1)
    seg_index = segment_of(token, ends)
    b_half = tok_ref[:, width : width + STATE].astype(f32)
    b_parts = jnp.concatenate(
        [jnp.where(seg_index == j, b_half, 0.0).astype(bf16) for j in range(REQS)], axis=1
    )
    out_ref[:, 0 : REQS * STATE] = dot_tn(scaled, b_parts).astype(bf16)
    member = (seg_index == lane % REQS).astype(f32).astype(bf16)
    total = None
    for piece in split(log_decay, 3):
        term = dot_tn(piece, member)
        total = term if total is None else total + term
    kept = jnp.exp(total)
    high = kept.astype(bf16).astype(f32)
    lane_h = lax.broadcasted_iota(jnp.int32, (heads, STATE), 1)
    parts = jnp.where(lane_h < REQS, high, jnp.where(lane_h < 2 * REQS, kept - high, 0.0))
    row_w = lax.broadcasted_iota(jnp.int32, (width, heads), 0)
    col_w = lax.broadcasted_iota(jnp.int32, (width, heads), 1)
    owner = (row_w // HEAD_DIM == col_w).astype(f32).astype(bf16)
    spread = dot(owner, parts.astype(bf16))
    row_s = lax.broadcasted_iota(jnp.int32, (width, STATE), 0)
    lane_s = lax.broadcasted_iota(jnp.int32, (width, STATE), 1)
    chosen = jnp.where(lane_s == row_s % ROWS, spread, 0.0).astype(bf16)
    out_ref[:, REQS * STATE :] = dot(chosen, jnp.ones((STATE, STATE), bf16)).astype(bf16)


def combine(hit_ref, place_ref, recv_ref, *refs):
    out_ref, held = refs[-2:]
    for s in range(recv_ref.shape[0]):
        block = recv_ref[s, :, 0 : SLOTS * STATE].astype(f32)
        for k in range(SLOTS):
            held[s * SLOTS + k] = block[:, k * STATE : (k + 1) * STATE]
    for s in range(recv_ref.shape[0]):
        block = recv_ref[s, :, SLOTS * STATE :].astype(f32)
        kept = block[:, REQS * STATE :]
        for j in range(REQS):
            prefix = held[hit_ref[s * REQS + j]]
            out_ref[s, :, j * STATE : (j + 1) * STATE] = prefix.astype(bf16)
            factor = kept[j : j + 1, :] + kept[REQS + j : REQS + j + 1, :]
            new = factor * prefix + block[:, j * STATE : (j + 1) * STATE]
            place = place_ref[s * REQS + j]
            start = pl.multiple_of((REQS + (place & 3)) * STATE, STATE)
            out_ref[place >> 2, :, pl.ds(start, STATE)] = new.astype(bf16)


def token_inner(me_ref, meta_ref, skip_ref, tok_ref, *refs):
    pair_refs, (base_ref, factor_ref, read_ref, gates, sems) = refs[:-5], refs[-5:]
    length = tok_ref.shape[0]
    heads = skip_ref.shape[1]
    width = heads * HEAD_DIM
    copies = fetch(me_ref[0], pair_refs, gates, sems)
    ends = segment_ends(meta_ref)
    step_size = jax.nn.softplus(tok_ref[:, width + STATE : width + STATE + heads].astype(f32))
    log_decay = -step_size * meta_ref[0:1, 0:heads]
    row = lax.broadcasted_iota(jnp.int32, (length, length), 0)
    column = lax.broadcasted_iota(jnp.int32, (length, length), 1)
    upto = (segment_of(row, ends) == segment_of(column, ends)) & (column <= row)
    running = exact_left(upto.astype(f32).astype(bf16), log_decay)
    spread = spread_heads(heads, width)
    decay = exact_right(jnp.exp(running), spread)
    undo = exact_right(jnp.exp(-running) * step_size, spread, 2)
    values = tok_ref[:, 0:width].astype(f32)
    b_half = tok_ref[:, width : width + STATE]
    for copy in copies:
        copy.wait()
    c_half = gates[:, width : width + STATE]
    c_wide = c_half.astype(f32)
    scores = jnp.where(upto, dot_nt(c_half, b_half), 0.0).astype(bf16)
    token = lax.broadcasted_iota(jnp.int32, (length, STATE), 0)
    seg_index = segment_of(token, ends)
    for j in range(REQS):
        read_ref[:, j * STATE : (j + 1) * STATE] = jnp.where(seg_index == j, c_wide, 0.0).astype(
            bf16
        )
    inner = dot(scores, (undo * values).astype(bf16))
    gate_in = gates[:, 0:width].astype(f32)
    gate = gate_in / (1.0 + jnp.exp(-gate_in))
    base_ref[...] = gate * (decay * inner + exact_right(skip_ref[...], spread) * values)
    factor_ref[...] = gate * decay


def finish(
    missing_ref, cache_ref, gain_ref, base_ref, factor_ref, read_ref, recv_ref,
    rows_ref, states_ref, rows, states, sems,
):
    missing = missing_ref[0]
    first = REQS * STATE
    copies = []
    for s in range(SLOTS):

        @pl.when(missing == s)
        def _():
            states[s] = cache_ref[s]

        if s < REQS:

            @pl.when(missing > s)
            def _():
                states[s] = recv_ref[:, first + s * STATE : first + (s + 1) * STATE].astype(f32)

        if s > 0:

            @pl.when(missing < s)
            def _():
                states[s] = recv_ref[:, first + (s - 1) * STATE : first + s * STATE].astype(f32)

        copies.append(pltpu.make_async_copy(states.at[s], states_ref.at[s], sems.at[s]))
        copies[-1].start()
    carried = dot_nt(read_ref[...], recv_ref[:, 0:first])
    gated = base_ref[...] + factor_ref[...] * carried
    square_mean = jnp.mean(gated * gated, axis=1, keepdims=True)
    rows[...] = (gated * lax.rsqrt(square_mean + 1e-05) * gain_ref[...]).astype(bf16)
    copies.append(pltpu.make_async_copy(rows, rows_ref, sems.at[SLOTS]))
    copies[-1].start()
    for copy in copies:
        copy.wait()


def gated_norm(values, gate_in, norm_weight):
    shaped = values.shape
    gated = values * jax.nn.silu(gate_in.astype(jnp.float32).reshape(shaped))
    square_mean = jnp.mean(gated * gated, axis=(2, 3), keepdims=True)
    normed = gated * lax.rsqrt(square_mean + 1e-05) * norm_weight.reshape(shaped[1:])
    return normed.reshape(shaped[0], -1).astype(jnp.bfloat16)


def decode_block(
    inputs, gate_in, b_proj, c_proj, step_raw, states, head_rates, skip_gain, norm_weight
):
    row_count = inputs.shape[0]
    head_count = step_raw.shape[1]
    groups = b_proj.shape[1] // STATE
    per_group = head_count // groups
    step_size = jax.nn.softplus(step_raw.astype(jnp.float32))
    factor = jnp.exp(-step_size * head_rates[None, :]).reshape(row_count, groups, per_group, 1, 1)
    values = inputs.astype(jnp.float32).reshape(row_count, groups, per_group, HEAD_DIM)
    b_group = b_proj.astype(jnp.float32).reshape(row_count, groups, STATE)
    c_group = c_proj.astype(jnp.float32).reshape(row_count, groups, STATE)
    written = (step_size.reshape(row_count, groups, per_group, 1) * values)[..., None] * b_group[
        :, :, None, None, :
    ]
    updated = factor * states.reshape(row_count, groups, per_group, HEAD_DIM, STATE) + written
    outputs = (
        jnp.einsum("rgkpn,rgn->rgkp", updated, c_group, precision=highest)
        + skip_gain.reshape(groups, per_group, 1) * values
    )
    return (
        gated_norm(outputs, gate_in, norm_weight),
        updated.reshape(row_count, head_count, HEAD_DIM, STATE),
    )


def local(
    pre_x,
    pre_z,
    pre_b,
    pre_c,
    pre_dt,
    suffix_lengths,
    prefix_hits,
    snapshot_slots,
    cache_states,
    dec_x,
    dec_z,
    dec_b,
    dec_c,
    dec_dt,
    dec_states,
    decay_rate,
    d_skip,
    norm_weight,
):
    n_head = lax.axis_size("head")
    n_serve = lax.axis_size("serve")
    rows = pre_x.shape[0]
    heads = cache_states.shape[1]
    width = heads * HEAD_DIM
    length = rows * n_head
    tiles = SLOTS + REQS + 1
    shape = jax.ShapeDtypeStruct

    def swap(value, axis):
        return lax.all_to_all(value, axis, split_axis=0, concat_axis=0, tiled=True)

    chips = n_head // 2
    with jax.named_scope("tokens"):
        first, meta = pl.pallas_call(
            pack_first,
            out_shape=(
                shape((n_head, rows, width + 2 * STATE), bf16),
                shape((8, STATE), f32),
            ),
            in_specs=[HBM] * 5,
            out_specs=(VMEM, VMEM),
            scratch_shapes=[
                pltpu.VMEM(pre_x.shape, bf16),
                pltpu.VMEM(pre_b.shape, bf16),
                pltpu.VMEM(pre_dt.shape, bf16),
                pltpu.VMEM((1, heads), f32),
                pltpu.VMEM(suffix_lengths.shape, jnp.int32),
                pltpu.SemaphoreType.DMA((5,)),
            ],
            compiler_params=params(56),
            cost_estimate=cost(0, 800_000),
        )(pre_x, pre_b, pre_dt, decay_rate.reshape(1, heads), suffix_lengths)
        tokens = swap(first, "head").reshape(length, width + 2 * STATE)
    with jax.named_scope("cache"):
        cache_rows = cache_states.reshape(SLOTS, width, STATE)
        send = pl.pallas_call(
            pack_cache,
            out_shape=shape((width, tiles * STATE), bf16),
            grid=(1,),
            in_specs=[VMEM],
            out_specs=pl.BlockSpec((width, SLOTS * STATE), lambda i: (0, 0)),
            compiler_params=params(),
            cost_estimate=cost(0, 1_600_000),
        )(cache_rows)
    with jax.named_scope("orders"):
        rank = jnp.sum(
            (snapshot_slots[None, :] < snapshot_slots[:, None]).astype(jnp.int32), axis=1
        )
        place = (rank // REQS) * 4 + rank % REQS
        serve_me = lax.axis_index("serve")
        missing = (
            sum(range(SLOTS))
            - jnp.sum(jnp.where(snapshot_slots // SLOTS == serve_me, snapshot_slots % SLOTS, 0))
        ).reshape(1)
        head_me = lax.axis_index("head").astype(jnp.int32).reshape(1)
    with jax.named_scope("local"):
        send = pl.pallas_call(
            local_state,
            out_shape=shape((width, tiles * STATE), bf16),
            grid=(1,),
            in_specs=[VMEM, VMEM, ANY],
            out_specs=pl.BlockSpec((width, SLOTS * STATE), lambda i: (0, 1)),
            input_output_aliases={2: 0},
            compiler_params=params(),
            cost_estimate=cost(300_000_000, 800_000),
        )(meta, tokens, send)
        pieces = swap(send.reshape(n_serve, ROWS, tiles * STATE), "serve")
    with jax.named_scope("gates"):
        keep, give = pl.pallas_call(
            pack_gates,
            out_shape=[shape((chips, rows, width + STATE), bf16)] * 2,
            in_specs=[SMEM, ANY] + [VMEM] * 2,
            out_specs=[VMEM] * 2,
            compiler_params=params(),
            cost_estimate=cost(0, 650_000),
        )(head_me, send, pre_z, pre_c)
        gates = exchange(keep, give, n_head)
    with jax.named_scope("combine"):
        answer = pl.pallas_call(
            combine,
            out_shape=shape((n_serve, ROWS, 2 * REQS * STATE), bf16),
            in_specs=[SMEM, SMEM, VMEM] + [ANY] * (chips - 1),
            out_specs=VMEM,
            scratch_shapes=[pltpu.VMEM((n_serve * SLOTS, ROWS, STATE), f32)],
            compiler_params=params(),
            cost_estimate=cost(0, 4_000_000),
        )(prefix_hits, place, pieces, *gates[1:])
        got = swap(answer, "serve").reshape(width, 2 * REQS * STATE)
    with jax.named_scope("inner"):
        base, factor, read = pl.pallas_call(
            token_inner,
            out_shape=(
                shape((length, width), f32),
                shape((length, width), f32),
                shape((length, REQS * STATE), bf16),
            ),
            in_specs=[SMEM] + [VMEM] * 3 + [ANY] * chips,
            out_specs=[VMEM] * 3,
            scratch_shapes=[
                pltpu.VMEM((length, width + STATE), bf16),
                pltpu.SemaphoreType.DMA((n_head,)),
            ],
            compiler_params=params(),
            cost_estimate=cost(400_000_000, 1_500_000),
        )(head_me, meta, d_skip.reshape(1, heads), tokens, *gates)
    dec_out, dec_new = decode_block(
        dec_x, dec_z, dec_b, dec_c, dec_dt, dec_states, decay_rate, d_skip, norm_weight
    )
    with jax.named_scope("outputs"):
        pre_out, cache_out = pl.pallas_call(
            finish,
            out_shape=(shape((length, width), bf16), shape((SLOTS, width, STATE), f32)),
            in_specs=[SMEM] + [VMEM] * 6,
            out_specs=(HBM, HBM),
            scratch_shapes=[
                pltpu.VMEM((length, width), bf16),
                pltpu.VMEM((SLOTS, width, STATE), f32),
                pltpu.SemaphoreType.DMA((SLOTS + 1,)),
            ],
            compiler_params=params(),
            cost_estimate=cost(200_000_000, 4_000_000),
        )(missing, cache_rows, norm_weight.reshape(1, width), base, factor, read, got)
        cache_out = cache_out.reshape(cache_states.shape)
    return (pre_out, cache_out, dec_out, dec_new)


def solution(mesh):
    return jax.shard_map(
        local,
        mesh=mesh,
        in_specs=(
            P(("serve", "head"), None),
            P(("serve", "head"), None),
            P(("serve", "head"), None),
            P(("serve", "head"), None),
            P(("serve", "head"), None),
            P("serve", None),
            P(),
            P(),
            P("serve", "head", None, None),
            P("serve", "head"),
            P("serve", "head"),
            P("serve", "head"),
            P("serve", "head"),
            P("serve", "head"),
            P("serve", "head", None, None),
            P("head"),
            P("head"),
            P("head"),
        ),
        out_specs=(
            P("serve", "head"),
            P("serve", "head", None, None),
            P("serve", "head"),
            P("serve", "head", None, None),
        ),
        check_vma=False,
    )
```

```python
import jax
import jax.numpy as jnp
from jax import lax
from jax.experimental import pallas as pl
from jax.experimental.pallas import tpu as pltpu
from jax.sharding import PartitionSpec as P

HEAD_DIM = 64
STATE = 128
REQS = 3
SLOTS = 4
ROWS = 8

f32 = jnp.float32
bf16 = jnp.bfloat16
highest = lax.Precision.HIGHEST

ANY = pl.BlockSpec(memory_space=pl.ANY)
HBM = pl.BlockSpec(memory_space=pltpu.HBM)
VMEM = pl.BlockSpec(memory_space=pltpu.VMEM)
SMEM = pl.BlockSpec(memory_space=pltpu.SMEM)


def params(mib=12):
    return pltpu.CompilerParams(vmem_limit_bytes=mib * 1024 * 1024)


def cost(flops, moved):
    return pl.CostEstimate(flops=flops, bytes_accessed=moved, transcendentals=0)


def dot(a, b):
    return jnp.dot(a, b, preferred_element_type=f32)


def dot_nt(a, b):
    return lax.dot_general(a, b, (((1,), (1,)), ((), ())), preferred_element_type=f32)


def dot_tn(a, b):
    return lax.dot_general(a, b, (((0,), (0,)), ((), ())), preferred_element_type=f32)


def split(value, parts):
    pieces = []
    for _ in range(parts):
        piece = value.astype(bf16)
        pieces.append(piece)
        value = value - piece.astype(f32)
    return pieces


def exact_left(mask, value, parts=3):
    total = None
    for piece in split(value, parts):
        term = dot(mask, piece)
        total = term if total is None else total + term
    return total


def exact_right(value, mask, parts=3):
    total = None
    for piece in split(value, parts):
        term = dot(piece, mask)
        total = term if total is None else total + term
    return total


def pack_first(
    x_ref, b_ref, dt_ref, rate_ref, len_ref, out_ref, meta_ref, xs, bs, steps, rates, lens, sems
):
    count = out_ref.shape[0]
    heads_dev = dt_ref.shape[1] // count
    width = x_ref.shape[1] // count
    copies = [
        pltpu.make_async_copy(src, dst, sems.at[i])
        for i, (src, dst) in enumerate(
            ((x_ref, xs), (b_ref, bs), (dt_ref, steps), (rate_ref, rates), (len_ref, lens))
        )
    ]
    for copy in copies:
        copy.start()
    for copy in copies:
        copy.wait()
    raw = steps[...].astype(f32)
    raw = jnp.concatenate([raw, jnp.zeros((raw.shape[0], STATE - raw.shape[1]), f32)], axis=1)
    for d in range(count):
        out_ref[d, :, 0:width] = xs[:, d * width : (d + 1) * width]
        out_ref[d, :, width : width + STATE] = bs[:, d * STATE : (d + 1) * STATE]
        mine = raw if d == 0 else pltpu.roll(raw, STATE - d * heads_dev, 1)
        out_ref[d, :, width + STATE : width + 2 * STATE] = mine.astype(bf16)
    meta_ref[...] = jnp.zeros_like(meta_ref)
    meta_ref[0:1, 0 : rates.shape[1]] = rates[...]
    meta_ref[1:2, 0:1] = lens[:, 0:1].astype(f32)
    meta_ref[2:3, 0:1] = (lens[:, 0:1] + lens[:, 1:2]).astype(f32)


def pack_gates(me_ref, after_ref, z_ref, c_ref, keep_ref, give_ref):
    del after_ref
    chips = keep_ref.shape[0]
    width = z_ref.shape[1] // (2 * chips)
    for side, ref in enumerate((keep_ref, give_ref)):
        for k in range(chips):
            peer = me_ref[0] ^ (2 * k + side)
            z_start = pl.multiple_of(peer * width, STATE)
            c_start = pl.multiple_of(peer * STATE, STATE)
            ref[k, :, 0:width] = z_ref[:, pl.ds(z_start, width)]
            ref[k, :, width : width + STATE] = c_ref[:, pl.ds(c_start, STATE)]


def pair_up(keep_ref, got_ref, *out_refs):
    for k, ref in enumerate(out_refs):
        ref[0] = keep_ref[k]
        ref[1] = got_ref[k]


def exchange(keep, give, n_head):
    chips = n_head // 2
    shape = jax.ShapeDtypeStruct((2,) + keep.shape[1:], bf16)
    got = lax.ppermute(give, "head", [(i, i ^ 1) for i in range(n_head)])
    pairs = pl.pallas_call(
        pair_up,
        out_shape=[shape] * chips,
        in_specs=[VMEM] * 2,
        out_specs=[VMEM] * chips,
        compiler_params=params(),
        cost_estimate=cost(0, 800_000),
    )(keep, got)
    return [pairs[0]] + [
        lax.ppermute(pairs[k], "head", [(i, i ^ (2 * k)) for i in range(n_head)])
        for k in range(1, chips)
    ]


def fetch(me, pair_refs, rows_ref, sems):
    rows = pair_refs[0].shape[1]
    copies = []
    for k, ref in enumerate(pair_refs):
        for side in range(2):
            start = pl.multiple_of((me ^ (2 * k + side)) * rows, rows)
            copies.append(
                pltpu.make_async_copy(
                    ref.at[side], rows_ref.at[pl.ds(start, rows), :], sems.at[2 * k + side]
                )
            )
    for copy in copies:
        copy.start()
    return copies


def pack_cache(cache_ref, out_ref):
    for s in range(SLOTS):
        out_ref[:, s * STATE : (s + 1) * STATE] = cache_ref[s].astype(bf16)


def segment_of(position, ends):
    return (position >= ends[0]).astype(jnp.int32) + (position >= ends[1]).astype(jnp.int32)


def segment_ends(meta_ref):
    return meta_ref[1:2, 0:1].astype(jnp.int32), meta_ref[2:3, 0:1].astype(jnp.int32)


def spread_heads(heads, width):
    row = lax.broadcasted_iota(jnp.int32, (heads, width), 0)
    column = lax.broadcasted_iota(jnp.int32, (heads, width), 1)
    return (row == column // (width // heads)).astype(bf16)


def local_state(meta_ref, tok_ref, send_ref, out_ref, made, sems):
    del send_ref
    length = tok_ref.shape[0]
    width = out_ref.shape[0]
    heads = width // HEAD_DIM
    ends = segment_ends(meta_ref)
    step_size = jax.nn.softplus(tok_ref[:, width + STATE : width + STATE + heads].astype(f32))
    log_decay = -step_size * meta_ref[0:1, 0:heads]
    row = lax.broadcasted_iota(jnp.int32, (length, length), 0)
    column = lax.broadcasted_iota(jnp.int32, (length, length), 1)
    later = (segment_of(row, ends) == segment_of(column, ends)) & (column > row)
    after = exact_left(later.astype(f32).astype(bf16), log_decay)
    weight = exact_right(jnp.exp(after) * step_size, spread_heads(heads, width), 2)
    scaled = (weight * tok_ref[:, 0:width].astype(f32)).astype(bf16)
    token = lax.broadcasted_iota(jnp.int32, (length, STATE), 0)
    lane = lax.broadcasted_iota(jnp.int32, (length, STATE), 1)
    seg_index = segment_of(token, ends)
    b_half = tok_ref[:, width : width + STATE].astype(f32)
    b_parts = jnp.concatenate(
        [jnp.where(seg_index == j, b_half, 0.0).astype(bf16) for j in range(REQS)], axis=1
    )
    made[:, 0 : REQS * STATE] = dot_tn(scaled, b_parts).astype(bf16)
    start, middle = SLOTS * STATE, (SLOTS + REQS) * STATE
    early = pltpu.make_async_copy(
        made.at[:, 0 : REQS * STATE], out_ref.at[:, start:middle], sems.at[0]
    )
    early.start()
    member = (seg_index == lane % REQS).astype(f32).astype(bf16)
    total = None
    for piece in split(log_decay, 3):
        term = dot_tn(piece, member)
        total = term if total is None else total + term
    kept = jnp.exp(total)
    high = kept.astype(bf16).astype(f32)
    lane_h = lax.broadcasted_iota(jnp.int32, (heads, STATE), 1)
    parts = jnp.where(lane_h < REQS, high, jnp.where(lane_h < 2 * REQS, kept - high, 0.0))
    row_w = lax.broadcasted_iota(jnp.int32, (width, heads), 0)
    col_w = lax.broadcasted_iota(jnp.int32, (width, heads), 1)
    owner = (row_w // HEAD_DIM == col_w).astype(f32).astype(bf16)
    spread = dot(owner, parts.astype(bf16))
    row_s = lax.broadcasted_iota(jnp.int32, (width, STATE), 0)
    lane_s = lax.broadcasted_iota(jnp.int32, (width, STATE), 1)
    chosen = jnp.where(lane_s == row_s % ROWS, spread, 0.0).astype(bf16)
    made[:, REQS * STATE :] = dot(chosen, jnp.ones((STATE, STATE), bf16)).astype(bf16)
    last = pltpu.make_async_copy(made.at[:, REQS * STATE :], out_ref.at[:, middle:], sems.at[1])
    last.start()
    early.wait()
    last.wait()


def combine(hit_ref, place_ref, recv_ref, *refs):
    out_ref = refs[-1]
    first = SLOTS * STATE
    for s in range(recv_ref.shape[0]):
        kept = recv_ref[s, :, first + REQS * STATE :].astype(f32)
        for j in range(REQS):
            hit = hit_ref[s * REQS + j]
            start = pl.multiple_of((hit & (SLOTS - 1)) * STATE, STATE)
            prefix = recv_ref[hit >> 2, :, pl.ds(start, STATE)]
            out_ref[s, :, j * STATE : (j + 1) * STATE] = prefix
            factor = kept[j : j + 1, :] + kept[REQS + j : REQS + j + 1, :]
            own = recv_ref[s, :, first + j * STATE : first + (j + 1) * STATE].astype(f32)
            new = factor * prefix.astype(f32) + own
            place = place_ref[s * REQS + j]
            start = pl.multiple_of((REQS + (place & 3)) * STATE, STATE)
            out_ref[place >> 2, :, pl.ds(start, STATE)] = new.astype(bf16)


def token_inner(me_ref, meta_ref, skip_ref, tok_ref, *refs):
    pair_refs, (base_ref, factor_ref, read_ref, gates, sems) = refs[:-5], refs[-5:]
    length = tok_ref.shape[0]
    heads = skip_ref.shape[1]
    width = heads * HEAD_DIM
    copies = fetch(me_ref[0], pair_refs, gates, sems)
    ends = segment_ends(meta_ref)
    step_size = jax.nn.softplus(tok_ref[:, width + STATE : width + STATE + heads].astype(f32))
    log_decay = -step_size * meta_ref[0:1, 0:heads]
    row = lax.broadcasted_iota(jnp.int32, (length, length), 0)
    column = lax.broadcasted_iota(jnp.int32, (length, length), 1)
    upto = (segment_of(row, ends) == segment_of(column, ends)) & (column <= row)
    running = exact_left(upto.astype(f32).astype(bf16), log_decay)
    spread = spread_heads(heads, width)
    decay = exact_right(jnp.exp(running), spread)
    undo = exact_right(jnp.exp(-running) * step_size, spread, 2)
    values = tok_ref[:, 0:width].astype(f32)
    b_half = tok_ref[:, width : width + STATE]
    for copy in copies:
        copy.wait()
    c_half = gates[:, width : width + STATE]
    c_wide = c_half.astype(f32)
    scores = jnp.where(upto, dot_nt(c_half, b_half), 0.0).astype(bf16)
    token = lax.broadcasted_iota(jnp.int32, (length, STATE), 0)
    seg_index = segment_of(token, ends)
    for j in range(REQS):
        read_ref[:, j * STATE : (j + 1) * STATE] = jnp.where(seg_index == j, c_wide, 0.0).astype(
            bf16
        )
    inner = dot(scores, (undo * values).astype(bf16))
    gate_in = gates[:, 0:width].astype(f32)
    gate = gate_in / (1.0 + jnp.exp(-gate_in))
    base_ref[...] = gate * (decay * inner + exact_right(skip_ref[...], spread) * values)
    factor_ref[...] = gate * decay


def finish(
    missing_ref, cache_ref, gain_ref, base_ref, factor_ref, read_ref, recv_ref,
    rows_ref, states_ref, rows, states, sems,
):
    missing = missing_ref[0]
    first = REQS * STATE
    copies = []
    for s in range(SLOTS):

        @pl.when(missing == s)
        def _():
            states[s] = cache_ref[s]

        if s < REQS:

            @pl.when(missing > s)
            def _():
                states[s] = recv_ref[:, first + s * STATE : first + (s + 1) * STATE].astype(f32)

        if s > 0:

            @pl.when(missing < s)
            def _():
                states[s] = recv_ref[:, first + (s - 1) * STATE : first + s * STATE].astype(f32)

        copies.append(pltpu.make_async_copy(states.at[s], states_ref.at[s], sems.at[s]))
        copies[-1].start()
    carried = dot_nt(read_ref[...], recv_ref[:, 0:first])
    gated = base_ref[...] + factor_ref[...] * carried
    square_mean = jnp.mean(gated * gated, axis=1, keepdims=True)
    rows[...] = (gated * lax.rsqrt(square_mean + 1e-05) * gain_ref[...]).astype(bf16)
    copies.append(pltpu.make_async_copy(rows, rows_ref, sems.at[SLOTS]))
    copies[-1].start()
    for copy in copies:
        copy.wait()


def gated_norm(values, gate_in, norm_weight):
    shaped = values.shape
    gated = values * jax.nn.silu(gate_in.astype(jnp.float32).reshape(shaped))
    square_mean = jnp.mean(gated * gated, axis=(2, 3), keepdims=True)
    normed = gated * lax.rsqrt(square_mean + 1e-05) * norm_weight.reshape(shaped[1:])
    return normed.reshape(shaped[0], -1).astype(jnp.bfloat16)


def decode_block(
    inputs, gate_in, b_proj, c_proj, step_raw, states, head_rates, skip_gain, norm_weight
):
    row_count = inputs.shape[0]
    head_count = step_raw.shape[1]
    groups = b_proj.shape[1] // STATE
    per_group = head_count // groups
    step_size = jax.nn.softplus(step_raw.astype(jnp.float32))
    factor = jnp.exp(-step_size * head_rates[None, :]).reshape(row_count, groups, per_group, 1, 1)
    values = inputs.astype(jnp.float32).reshape(row_count, groups, per_group, HEAD_DIM)
    b_group = b_proj.astype(jnp.float32).reshape(row_count, groups, STATE)
    c_group = c_proj.astype(jnp.float32).reshape(row_count, groups, STATE)
    written = (step_size.reshape(row_count, groups, per_group, 1) * values)[..., None] * b_group[
        :, :, None, None, :
    ]
    updated = factor * states.reshape(row_count, groups, per_group, HEAD_DIM, STATE) + written
    outputs = (
        jnp.einsum("rgkpn,rgn->rgkp", updated, c_group, precision=highest)
        + skip_gain.reshape(groups, per_group, 1) * values
    )
    return (
        gated_norm(outputs, gate_in, norm_weight),
        updated.reshape(row_count, head_count, HEAD_DIM, STATE),
    )


def local(
    pre_x,
    pre_z,
    pre_b,
    pre_c,
    pre_dt,
    suffix_lengths,
    prefix_hits,
    snapshot_slots,
    cache_states,
    dec_x,
    dec_z,
    dec_b,
    dec_c,
    dec_dt,
    dec_states,
    decay_rate,
    d_skip,
    norm_weight,
):
    n_head = lax.axis_size("head")
    n_serve = lax.axis_size("serve")
    rows = pre_x.shape[0]
    heads = cache_states.shape[1]
    width = heads * HEAD_DIM
    length = rows * n_head
    tiles = SLOTS + REQS + 1
    shape = jax.ShapeDtypeStruct

    def swap(value, axis):
        return lax.all_to_all(value, axis, split_axis=0, concat_axis=0, tiled=True)

    chips = n_head // 2
    with jax.named_scope("tokens"):
        first, meta = pl.pallas_call(
            pack_first,
            out_shape=(
                shape((n_head, rows, width + 2 * STATE), bf16),
                shape((8, STATE), f32),
            ),
            in_specs=[HBM] * 5,
            out_specs=(VMEM, VMEM),
            scratch_shapes=[
                pltpu.VMEM(pre_x.shape, bf16),
                pltpu.VMEM(pre_b.shape, bf16),
                pltpu.VMEM(pre_dt.shape, bf16),
                pltpu.VMEM((1, heads), f32),
                pltpu.VMEM(suffix_lengths.shape, jnp.int32),
                pltpu.SemaphoreType.DMA((5,)),
            ],
            compiler_params=params(56),
            cost_estimate=cost(0, 800_000),
        )(pre_x, pre_b, pre_dt, decay_rate.reshape(1, heads), suffix_lengths)
        tokens = swap(first, "head").reshape(length, width + 2 * STATE)
    with jax.named_scope("cache"):
        cache_rows = cache_states.reshape(SLOTS, width, STATE)
        send = pl.pallas_call(
            pack_cache,
            out_shape=shape((width, tiles * STATE), bf16),
            grid=(1,),
            in_specs=[VMEM],
            out_specs=pl.BlockSpec((width, SLOTS * STATE), lambda i: (0, 0)),
            compiler_params=params(),
            cost_estimate=cost(0, 1_600_000),
        )(cache_rows)
    with jax.named_scope("orders"):
        rank = jnp.sum(
            (snapshot_slots[None, :] < snapshot_slots[:, None]).astype(jnp.int32), axis=1
        )
        place = (rank // REQS) * 4 + rank % REQS
        serve_me = lax.axis_index("serve")
        missing = (
            sum(range(SLOTS))
            - jnp.sum(jnp.where(snapshot_slots // SLOTS == serve_me, snapshot_slots % SLOTS, 0))
        ).reshape(1)
        head_me = lax.axis_index("head").astype(jnp.int32).reshape(1)
    with jax.named_scope("local"):
        send = pl.pallas_call(
            local_state,
            out_shape=shape((width, tiles * STATE), bf16),
            in_specs=[VMEM, VMEM, HBM],
            out_specs=HBM,
            scratch_shapes=[
                pltpu.VMEM((width, (REQS + 1) * STATE), bf16),
                pltpu.SemaphoreType.DMA((2,)),
            ],
            input_output_aliases={2: 0},
            compiler_params=params(),
            cost_estimate=cost(300_000_000, 800_000),
        )(meta, tokens, send)
        pieces = swap(send.reshape(n_serve, ROWS, tiles * STATE), "serve")
    with jax.named_scope("gates"):
        keep, give = pl.pallas_call(
            pack_gates,
            out_shape=[shape((chips, rows, width + STATE), bf16)] * 2,
            in_specs=[SMEM, ANY] + [VMEM] * 2,
            out_specs=[VMEM] * 2,
            compiler_params=params(),
            cost_estimate=cost(0, 650_000),
        )(head_me, send, pre_z, pre_c)
        gates = exchange(keep, give, n_head)
    with jax.named_scope("combine"):
        answer = pl.pallas_call(
            combine,
            out_shape=shape((n_serve, ROWS, 2 * REQS * STATE), bf16),
            in_specs=[SMEM, SMEM, VMEM] + [ANY] * (chips - 1),
            out_specs=VMEM,
            compiler_params=params(),
            cost_estimate=cost(0, 4_000_000),
        )(prefix_hits, place, pieces, *gates[1:])
        got = swap(answer, "serve").reshape(width, 2 * REQS * STATE)
    with jax.named_scope("inner"):
        base, factor, read = pl.pallas_call(
            token_inner,
            out_shape=(
                shape((length, width), f32),
                shape((length, width), f32),
                shape((length, REQS * STATE), bf16),
            ),
            in_specs=[SMEM] + [VMEM] * 3 + [ANY] * chips,
            out_specs=[VMEM] * 3,
            scratch_shapes=[
                pltpu.VMEM((length, width + STATE), bf16),
                pltpu.SemaphoreType.DMA((n_head,)),
            ],
            compiler_params=params(),
            cost_estimate=cost(400_000_000, 1_500_000),
        )(head_me, meta, d_skip.reshape(1, heads), tokens, *gates)
    dec_out, dec_new = decode_block(
        dec_x, dec_z, dec_b, dec_c, dec_dt, dec_states, decay_rate, d_skip, norm_weight
    )
    with jax.named_scope("outputs"):
        pre_out, cache_out = pl.pallas_call(
            finish,
            out_shape=(shape((length, width), bf16), shape((SLOTS, width, STATE), f32)),
            in_specs=[SMEM] + [VMEM] * 6,
            out_specs=(HBM, HBM),
            scratch_shapes=[
                pltpu.VMEM((length, width), bf16),
                pltpu.VMEM((SLOTS, width, STATE), f32),
                pltpu.SemaphoreType.DMA((SLOTS + 1,)),
            ],
            compiler_params=params(),
            cost_estimate=cost(200_000_000, 4_000_000),
        )(missing, cache_rows, norm_weight.reshape(1, width), base, factor, read, got)
        cache_out = cache_out.reshape(cache_states.shape)
    return (pre_out, cache_out, dec_out, dec_new)


def solution(mesh):
    return jax.shard_map(
        local,
        mesh=mesh,
        in_specs=(
            P(("serve", "head"), None),
            P(("serve", "head"), None),
            P(("serve", "head"), None),
            P(("serve", "head"), None),
            P(("serve", "head"), None),
            P("serve", None),
            P(),
            P(),
            P("serve", "head", None, None),
            P("serve", "head"),
            P("serve", "head"),
            P("serve", "head"),
            P("serve", "head"),
            P("serve", "head"),
            P("serve", "head", None, None),
            P("head"),
            P("head"),
            P("head"),
        ),
        out_specs=(
            P("serve", "head"),
            P("serve", "head", None, None),
            P("serve", "head"),
            P("serve", "head", None, None),
        ),
        check_vma=False,
    )
```

```python
import jax
import jax.numpy as jnp
from jax import lax
from jax.experimental import pallas as pl
from jax.experimental.pallas import tpu as pltpu
from jax.sharding import PartitionSpec as P

HEAD_DIM = 64
STATE = 128
REQS = 3
SLOTS = 4
ROWS = 8

f32 = jnp.float32
bf16 = jnp.bfloat16
highest = lax.Precision.HIGHEST

ANY = pl.BlockSpec(memory_space=pl.ANY)
HBM = pl.BlockSpec(memory_space=pltpu.HBM)
VMEM = pl.BlockSpec(memory_space=pltpu.VMEM)
SMEM = pl.BlockSpec(memory_space=pltpu.SMEM)


def params(mib=12):
    return pltpu.CompilerParams(vmem_limit_bytes=mib * 1024 * 1024)


def cost(flops, moved):
    return pl.CostEstimate(flops=flops, bytes_accessed=moved, transcendentals=0)


def dot(a, b):
    return jnp.dot(a, b, preferred_element_type=f32)


def dot_nt(a, b):
    return lax.dot_general(a, b, (((1,), (1,)), ((), ())), preferred_element_type=f32)


def dot_tn(a, b):
    return lax.dot_general(a, b, (((0,), (0,)), ((), ())), preferred_element_type=f32)


def split(value, parts):
    pieces = []
    for _ in range(parts):
        piece = value.astype(bf16)
        pieces.append(piece)
        value = value - piece.astype(f32)
    return pieces


def exact_left(mask, value, parts=3):
    total = None
    for piece in split(value, parts):
        term = dot(mask, piece)
        total = term if total is None else total + term
    return total


def exact_right(value, mask, parts=3):
    total = None
    for piece in split(value, parts):
        term = dot(piece, mask)
        total = term if total is None else total + term
    return total


def pack_first(
    x_ref, b_ref, dt_ref, rate_ref, len_ref, out_ref, meta_ref,
    xs, bs, steps, rates, lens, made, sems, out_sems,
):
    count = out_ref.shape[0]
    heads_dev = dt_ref.shape[1] // count
    width = x_ref.shape[1] // count
    copies = [
        pltpu.make_async_copy(src, dst, sems.at[i])
        for i, (src, dst) in enumerate(
            ((dt_ref, steps), (b_ref, bs), (x_ref, xs), (rate_ref, rates), (len_ref, lens))
        )
    ]
    for copy in copies:
        copy.start()
    copies[0].wait()
    raw = steps[...].astype(f32)
    raw = jnp.concatenate([raw, jnp.zeros((raw.shape[0], STATE - raw.shape[1]), f32)], axis=1)
    for d in range(count):
        mine = raw if d == 0 else pltpu.roll(raw, STATE - d * heads_dev, 1)
        made[d, :, width + STATE : width + 2 * STATE] = mine.astype(bf16)
    copies[1].wait()
    for d in range(count):
        made[d, :, width : width + STATE] = bs[:, d * STATE : (d + 1) * STATE]
    copies[2].wait()
    leaving = []
    for d in range(count):
        made[d, :, 0:width] = xs[:, d * width : (d + 1) * width]
        leaving.append(pltpu.make_async_copy(made.at[d], out_ref.at[d], out_sems.at[d]))
        leaving[-1].start()
    copies[3].wait()
    copies[4].wait()
    meta_ref[...] = jnp.zeros_like(meta_ref)
    meta_ref[0:1, 0 : rates.shape[1]] = rates[...]
    meta_ref[1:2, 0:1] = lens[:, 0:1].astype(f32)
    meta_ref[2:3, 0:1] = (lens[:, 0:1] + lens[:, 1:2]).astype(f32)
    for copy in leaving:
        copy.wait()


def pack_gates(me_ref, after_ref, z_ref, c_ref, keep_ref, give_ref):
    del after_ref
    chips = keep_ref.shape[0]
    width = z_ref.shape[1] // (2 * chips)
    for side, ref in enumerate((keep_ref, give_ref)):
        for k in range(chips):
            peer = me_ref[0] ^ (2 * k + side)
            z_start = pl.multiple_of(peer * width, STATE)
            c_start = pl.multiple_of(peer * STATE, STATE)
            ref[k, :, 0:width] = z_ref[:, pl.ds(z_start, width)]
            ref[k, :, width : width + STATE] = c_ref[:, pl.ds(c_start, STATE)]


def pair_up(keep_ref, got_ref, *out_refs):
    for k, ref in enumerate(out_refs):
        ref[0] = keep_ref[k]
        ref[1] = got_ref[k]


def exchange(keep, give, n_head):
    chips = n_head // 2
    shape = jax.ShapeDtypeStruct((2,) + keep.shape[1:], bf16)
    got = lax.ppermute(give, "head", [(i, i ^ 1) for i in range(n_head)])
    pairs = pl.pallas_call(
        pair_up,
        out_shape=[shape] * chips,
        in_specs=[VMEM] * 2,
        out_specs=[VMEM] * chips,
        compiler_params=params(),
        cost_estimate=cost(0, 800_000),
    )(keep, got)
    return [pairs[0]] + [
        lax.ppermute(pairs[k], "head", [(i, i ^ (2 * k)) for i in range(n_head)])
        for k in range(1, chips)
    ]


def fetch(me, pair_refs, rows_ref, sems):
    rows = pair_refs[0].shape[1]
    copies = []
    for k, ref in enumerate(pair_refs):
        for side in range(2):
            start = pl.multiple_of((me ^ (2 * k + side)) * rows, rows)
            copies.append(
                pltpu.make_async_copy(
                    ref.at[side], rows_ref.at[pl.ds(start, rows), :], sems.at[2 * k + side]
                )
            )
    for copy in copies:
        copy.start()
    return copies


def pack_cache(cache_ref, out_ref):
    for s in range(SLOTS):
        out_ref[:, s * STATE : (s + 1) * STATE] = cache_ref[s].astype(bf16)


def segment_of(position, ends):
    return (position >= ends[0]).astype(jnp.int32) + (position >= ends[1]).astype(jnp.int32)


def segment_ends(meta_ref):
    return meta_ref[1:2, 0:1].astype(jnp.int32), meta_ref[2:3, 0:1].astype(jnp.int32)


def spread_heads(heads, width):
    row = lax.broadcasted_iota(jnp.int32, (heads, width), 0)
    column = lax.broadcasted_iota(jnp.int32, (heads, width), 1)
    return (row == column // (width // heads)).astype(bf16)


def local_state(meta_ref, tok_ref, send_ref, out_ref, made, sems):
    del send_ref
    length = tok_ref.shape[0]
    width = out_ref.shape[0]
    heads = width // HEAD_DIM
    ends = segment_ends(meta_ref)
    step_size = jax.nn.softplus(tok_ref[:, width + STATE : width + STATE + heads].astype(f32))
    log_decay = -step_size * meta_ref[0:1, 0:heads]
    row = lax.broadcasted_iota(jnp.int32, (length, length), 0)
    column = lax.broadcasted_iota(jnp.int32, (length, length), 1)
    later = (segment_of(row, ends) == segment_of(column, ends)) & (column > row)
    after = exact_left(later.astype(f32).astype(bf16), log_decay)
    weight = exact_right(jnp.exp(after) * step_size, spread_heads(heads, width), 2)
    scaled = (weight * tok_ref[:, 0:width].astype(f32)).astype(bf16)
    token = lax.broadcasted_iota(jnp.int32, (length, STATE), 0)
    lane = lax.broadcasted_iota(jnp.int32, (length, STATE), 1)
    seg_index = segment_of(token, ends)
    b_half = tok_ref[:, width : width + STATE].astype(f32)
    b_parts = jnp.concatenate(
        [jnp.where(seg_index == j, b_half, 0.0).astype(bf16) for j in range(REQS)], axis=1
    )
    made[:, 0 : REQS * STATE] = dot_tn(scaled, b_parts).astype(bf16)
    start, middle = SLOTS * STATE, (SLOTS + REQS) * STATE
    early = pltpu.make_async_copy(
        made.at[:, 0 : REQS * STATE], out_ref.at[:, start:middle], sems.at[0]
    )
    early.start()
    member = (seg_index == lane % REQS).astype(f32).astype(bf16)
    total = None
    for piece in split(log_decay, 3):
        term = dot_tn(piece, member)
        total = term if total is None else total + term
    kept = jnp.exp(total)
    high = kept.astype(bf16).astype(f32)
    lane_h = lax.broadcasted_iota(jnp.int32, (heads, STATE), 1)
    parts = jnp.where(lane_h < REQS, high, jnp.where(lane_h < 2 * REQS, kept - high, 0.0))
    row_w = lax.broadcasted_iota(jnp.int32, (width, heads), 0)
    col_w = lax.broadcasted_iota(jnp.int32, (width, heads), 1)
    owner = (row_w // HEAD_DIM == col_w).astype(f32).astype(bf16)
    spread = dot(owner, parts.astype(bf16))
    row_s = lax.broadcasted_iota(jnp.int32, (width, STATE), 0)
    lane_s = lax.broadcasted_iota(jnp.int32, (width, STATE), 1)
    chosen = jnp.where(lane_s == row_s % ROWS, spread, 0.0).astype(bf16)
    made[:, REQS * STATE :] = dot(chosen, jnp.ones((STATE, STATE), bf16)).astype(bf16)
    last = pltpu.make_async_copy(made.at[:, REQS * STATE :], out_ref.at[:, middle:], sems.at[1])
    last.start()
    early.wait()
    last.wait()


def combine(hit_ref, place_ref, recv_ref, *refs):
    out_ref, held, picked, made, sems = refs[-5:]
    first, half = SLOTS * STATE, REQS * STATE
    for s in range(recv_ref.shape[0]):
        block = recv_ref[s, :, 0:first].astype(f32)
        for k in range(SLOTS):
            held[s * SLOTS + k] = block[:, k * STATE : (k + 1) * STATE]
    for s in range(recv_ref.shape[0]):
        for j in range(REQS):
            picked[s, :, j * STATE : (j + 1) * STATE] = held[hit_ref[s * REQS + j]].astype(bf16)
    early = pltpu.make_async_copy(picked, out_ref.at[:, :, 0:half], sems.at[0])
    early.start()
    for s in range(recv_ref.shape[0]):
        block = recv_ref[s, :, first:].astype(f32)
        prefix = picked[s].astype(f32)
        kept = block[:, half:]
        for j in range(REQS):
            columns = slice(j * STATE, (j + 1) * STATE)
            factor = kept[j : j + 1, :] + kept[REQS + j : REQS + j + 1, :]
            new = factor * prefix[:, columns] + block[:, columns]
            place = place_ref[s * REQS + j]
            start = pl.multiple_of((place & 3) * STATE, STATE)
            made[place >> 2, :, pl.ds(start, STATE)] = new.astype(bf16)
    last = pltpu.make_async_copy(made, out_ref.at[:, :, half:], sems.at[1])
    last.start()
    early.wait()
    last.wait()


def token_inner(me_ref, meta_ref, skip_ref, tok_ref, *refs):
    pair_refs, (base_ref, factor_ref, read_ref, gates, sems) = refs[:-5], refs[-5:]
    length = tok_ref.shape[0]
    heads = skip_ref.shape[1]
    width = heads * HEAD_DIM
    copies = fetch(me_ref[0], pair_refs, gates, sems)
    ends = segment_ends(meta_ref)
    step_size = jax.nn.softplus(tok_ref[:, width + STATE : width + STATE + heads].astype(f32))
    log_decay = -step_size * meta_ref[0:1, 0:heads]
    row = lax.broadcasted_iota(jnp.int32, (length, length), 0)
    column = lax.broadcasted_iota(jnp.int32, (length, length), 1)
    upto = (segment_of(row, ends) == segment_of(column, ends)) & (column <= row)
    running = exact_left(upto.astype(f32).astype(bf16), log_decay)
    spread = spread_heads(heads, width)
    decay = exact_right(jnp.exp(running), spread)
    undo = exact_right(jnp.exp(-running) * step_size, spread, 2)
    values = tok_ref[:, 0:width].astype(f32)
    b_half = tok_ref[:, width : width + STATE]
    for copy in copies:
        copy.wait()
    c_half = gates[:, width : width + STATE]
    c_wide = c_half.astype(f32)
    scores = jnp.where(upto, dot_nt(c_half, b_half), 0.0).astype(bf16)
    token = lax.broadcasted_iota(jnp.int32, (length, STATE), 0)
    seg_index = segment_of(token, ends)
    for j in range(REQS):
        read_ref[:, j * STATE : (j + 1) * STATE] = jnp.where(seg_index == j, c_wide, 0.0).astype(
            bf16
        )
    inner = dot(scores, (undo * values).astype(bf16))
    gate_in = gates[:, 0:width].astype(f32)
    gate = gate_in / (1.0 + jnp.exp(-gate_in))
    base_ref[...] = gate * (decay * inner + exact_right(skip_ref[...], spread) * values)
    factor_ref[...] = gate * decay


def finish(
    missing_ref, cache_ref, gain_ref, base_ref, factor_ref, read_ref, recv_ref,
    rows_ref, states_ref, rows, states, sems,
):
    missing = missing_ref[0]
    first = REQS * STATE
    copies = []
    for s in range(SLOTS):

        @pl.when(missing == s)
        def _():
            states[s] = cache_ref[s]

        if s < REQS:

            @pl.when(missing > s)
            def _():
                states[s] = recv_ref[:, first + s * STATE : first + (s + 1) * STATE].astype(f32)

        if s > 0:

            @pl.when(missing < s)
            def _():
                states[s] = recv_ref[:, first + (s - 1) * STATE : first + s * STATE].astype(f32)

        copies.append(pltpu.make_async_copy(states.at[s], states_ref.at[s], sems.at[s]))
        copies[-1].start()
    carried = dot_nt(read_ref[...], recv_ref[:, 0:first])
    gated = base_ref[...] + factor_ref[...] * carried
    square_mean = jnp.mean(gated * gated, axis=1, keepdims=True)
    rows[...] = (gated * lax.rsqrt(square_mean + 1e-05) * gain_ref[...]).astype(bf16)
    copies.append(pltpu.make_async_copy(rows, rows_ref, sems.at[SLOTS]))
    copies[-1].start()
    for copy in copies:
        copy.wait()


def gated_norm(values, gate_in, norm_weight):
    shaped = values.shape
    gated = values * jax.nn.silu(gate_in.astype(jnp.float32).reshape(shaped))
    square_mean = jnp.mean(gated * gated, axis=(2, 3), keepdims=True)
    normed = gated * lax.rsqrt(square_mean + 1e-05) * norm_weight.reshape(shaped[1:])
    return normed.reshape(shaped[0], -1).astype(jnp.bfloat16)


def decode_block(
    inputs, gate_in, b_proj, c_proj, step_raw, states, head_rates, skip_gain, norm_weight
):
    row_count = inputs.shape[0]
    head_count = step_raw.shape[1]
    groups = b_proj.shape[1] // STATE
    per_group = head_count // groups
    step_size = jax.nn.softplus(step_raw.astype(jnp.float32))
    factor = jnp.exp(-step_size * head_rates[None, :]).reshape(row_count, groups, per_group, 1, 1)
    values = inputs.astype(jnp.float32).reshape(row_count, groups, per_group, HEAD_DIM)
    b_group = b_proj.astype(jnp.float32).reshape(row_count, groups, STATE)
    c_group = c_proj.astype(jnp.float32).reshape(row_count, groups, STATE)
    written = (step_size.reshape(row_count, groups, per_group, 1) * values)[..., None] * b_group[
        :, :, None, None, :
    ]
    updated = factor * states.reshape(row_count, groups, per_group, HEAD_DIM, STATE) + written
    outputs = (
        jnp.einsum("rgkpn,rgn->rgkp", updated, c_group, precision=highest)
        + skip_gain.reshape(groups, per_group, 1) * values
    )
    return (
        gated_norm(outputs, gate_in, norm_weight),
        updated.reshape(row_count, head_count, HEAD_DIM, STATE),
    )


def local(
    pre_x,
    pre_z,
    pre_b,
    pre_c,
    pre_dt,
    suffix_lengths,
    prefix_hits,
    snapshot_slots,
    cache_states,
    dec_x,
    dec_z,
    dec_b,
    dec_c,
    dec_dt,
    dec_states,
    decay_rate,
    d_skip,
    norm_weight,
):
    n_head = lax.axis_size("head")
    n_serve = lax.axis_size("serve")
    rows = pre_x.shape[0]
    heads = cache_states.shape[1]
    width = heads * HEAD_DIM
    length = rows * n_head
    tiles = SLOTS + REQS + 1
    shape = jax.ShapeDtypeStruct

    def swap(value, axis):
        return lax.all_to_all(value, axis, split_axis=0, concat_axis=0, tiled=True)

    chips = n_head // 2
    with jax.named_scope("tokens"):
        first, meta = pl.pallas_call(
            pack_first,
            out_shape=(
                shape((n_head, rows, width + 2 * STATE), bf16),
                shape((8, STATE), f32),
            ),
            in_specs=[HBM] * 5,
            out_specs=(HBM, VMEM),
            scratch_shapes=[
                pltpu.VMEM(pre_x.shape, bf16),
                pltpu.VMEM(pre_b.shape, bf16),
                pltpu.VMEM(pre_dt.shape, bf16),
                pltpu.VMEM((1, heads), f32),
                pltpu.VMEM(suffix_lengths.shape, jnp.int32),
                pltpu.VMEM((n_head, rows, width + 2 * STATE), bf16),
                pltpu.SemaphoreType.DMA((5,)),
                pltpu.SemaphoreType.DMA((n_head,)),
            ],
            compiler_params=params(56),
            cost_estimate=cost(0, 800_000),
        )(pre_x, pre_b, pre_dt, decay_rate.reshape(1, heads), suffix_lengths)
        tokens = swap(first, "head").reshape(length, width + 2 * STATE)
    with jax.named_scope("cache"):
        cache_rows = cache_states.reshape(SLOTS, width, STATE)
        send = pl.pallas_call(
            pack_cache,
            out_shape=shape((width, tiles * STATE), bf16),
            grid=(1,),
            in_specs=[VMEM],
            out_specs=pl.BlockSpec((width, SLOTS * STATE), lambda i: (0, 0)),
            compiler_params=params(),
            cost_estimate=cost(0, 1_600_000),
        )(cache_rows)
    with jax.named_scope("orders"):
        rank = jnp.sum(
            (snapshot_slots[None, :] < snapshot_slots[:, None]).astype(jnp.int32), axis=1
        )
        place = (rank // REQS) * 4 + rank % REQS
        serve_me = lax.axis_index("serve")
        missing = (
            sum(range(SLOTS))
            - jnp.sum(jnp.where(snapshot_slots // SLOTS == serve_me, snapshot_slots % SLOTS, 0))
        ).reshape(1)
        head_me = lax.axis_index("head").astype(jnp.int32).reshape(1)
    with jax.named_scope("local"):
        send = pl.pallas_call(
            local_state,
            out_shape=shape((width, tiles * STATE), bf16),
            in_specs=[VMEM, VMEM, HBM],
            out_specs=HBM,
            scratch_shapes=[
                pltpu.VMEM((width, (REQS + 1) * STATE), bf16),
                pltpu.SemaphoreType.DMA((2,)),
            ],
            input_output_aliases={2: 0},
            compiler_params=params(),
            cost_estimate=cost(300_000_000, 800_000),
        )(meta, tokens, send)
        pieces = swap(send.reshape(n_serve, ROWS, tiles * STATE), "serve")
    with jax.named_scope("gates"):
        keep, give = pl.pallas_call(
            pack_gates,
            out_shape=[shape((chips, rows, width + STATE), bf16)] * 2,
            in_specs=[SMEM, ANY] + [VMEM] * 2,
            out_specs=[VMEM] * 2,
            compiler_params=params(),
            cost_estimate=cost(0, 650_000),
        )(head_me, send, pre_z, pre_c)
        gates = exchange(keep, give, n_head)
    with jax.named_scope("combine"):
        answer = pl.pallas_call(
            combine,
            out_shape=shape((n_serve, ROWS, 2 * REQS * STATE), bf16),
            in_specs=[SMEM, SMEM, VMEM] + [ANY] * (chips - 1),
            out_specs=HBM,
            scratch_shapes=[
                pltpu.VMEM((n_serve * SLOTS, ROWS, STATE), f32),
                pltpu.VMEM((n_serve, ROWS, REQS * STATE), bf16),
                pltpu.VMEM((n_serve, ROWS, REQS * STATE), bf16),
                pltpu.SemaphoreType.DMA((2,)),
            ],
            compiler_params=params(),
            cost_estimate=cost(0, 4_000_000),
        )(prefix_hits, place, pieces, *gates[1:])
        got = swap(answer, "serve").reshape(width, 2 * REQS * STATE)
    with jax.named_scope("inner"):
        base, factor, read = pl.pallas_call(
            token_inner,
            out_shape=(
                shape((length, width), f32),
                shape((length, width), f32),
                shape((length, REQS * STATE), bf16),
            ),
            in_specs=[SMEM] + [VMEM] * 3 + [ANY] * chips,
            out_specs=[VMEM] * 3,
            scratch_shapes=[
                pltpu.VMEM((length, width + STATE), bf16),
                pltpu.SemaphoreType.DMA((n_head,)),
            ],
            compiler_params=params(),
            cost_estimate=cost(400_000_000, 1_500_000),
        )(head_me, meta, d_skip.reshape(1, heads), tokens, *gates)
    dec_out, dec_new = decode_block(
        dec_x, dec_z, dec_b, dec_c, dec_dt, dec_states, decay_rate, d_skip, norm_weight
    )
    with jax.named_scope("outputs"):
        pre_out, cache_out = pl.pallas_call(
            finish,
            out_shape=(shape((length, width), bf16), shape((SLOTS, width, STATE), f32)),
            in_specs=[SMEM] + [VMEM] * 6,
            out_specs=(HBM, HBM),
            scratch_shapes=[
                pltpu.VMEM((length, width), bf16),
                pltpu.VMEM((SLOTS, width, STATE), f32),
                pltpu.SemaphoreType.DMA((SLOTS + 1,)),
            ],
            compiler_params=params(),
            cost_estimate=cost(200_000_000, 4_000_000),
        )(missing, cache_rows, norm_weight.reshape(1, width), base, factor, read, got)
        cache_out = cache_out.reshape(cache_states.shape)
    return (pre_out, cache_out, dec_out, dec_new)


def solution(mesh):
    return jax.shard_map(
        local,
        mesh=mesh,
        in_specs=(
            P(("serve", "head"), None),
            P(("serve", "head"), None),
            P(("serve", "head"), None),
            P(("serve", "head"), None),
            P(("serve", "head"), None),
            P("serve", None),
            P(),
            P(),
            P("serve", "head", None, None),
            P("serve", "head"),
            P("serve", "head"),
            P("serve", "head"),
            P("serve", "head"),
            P("serve", "head"),
            P("serve", "head", None, None),
            P("head"),
            P("head"),
            P("head"),
        ),
        out_specs=(
            P("serve", "head"),
            P("serve", "head", None, None),
            P("serve", "head"),
            P("serve", "head", None, None),
        ),
        check_vma=False,
    )
```

```python
import jax
import jax.numpy as jnp
from jax import lax
from jax.experimental import pallas as pl
from jax.experimental.pallas import tpu as pltpu
from jax.sharding import PartitionSpec as P

HEAD_DIM = 64
STATE = 128
REQS = 3
SLOTS = 4
ROWS = 8

f32 = jnp.float32
bf16 = jnp.bfloat16
highest = lax.Precision.HIGHEST

ANY = pl.BlockSpec(memory_space=pl.ANY)
HBM = pl.BlockSpec(memory_space=pltpu.HBM)
VMEM = pl.BlockSpec(memory_space=pltpu.VMEM)
SMEM = pl.BlockSpec(memory_space=pltpu.SMEM)


def params(mib=12):
    return pltpu.CompilerParams(vmem_limit_bytes=mib * 1024 * 1024)


def cost(flops, moved):
    return pl.CostEstimate(flops=flops, bytes_accessed=moved, transcendentals=0)


def dot(a, b):
    return jnp.dot(a, b, preferred_element_type=f32)


def dot_nt(a, b):
    return lax.dot_general(a, b, (((1,), (1,)), ((), ())), preferred_element_type=f32)


def dot_tn(a, b):
    return lax.dot_general(a, b, (((0,), (0,)), ((), ())), preferred_element_type=f32)


def split(value, parts):
    pieces = []
    for _ in range(parts):
        piece = value.astype(bf16)
        pieces.append(piece)
        value = value - piece.astype(f32)
    return pieces


def exact_left(mask, value, parts=3):
    total = None
    for piece in split(value, parts):
        term = dot(mask, piece)
        total = term if total is None else total + term
    return total


def exact_right(value, mask, parts=3):
    total = None
    for piece in split(value, parts):
        term = dot(piece, mask)
        total = term if total is None else total + term
    return total


def pack_first(
    x_ref, b_ref, dt_ref, rate_ref, len_ref, out_ref, meta_ref, xs, bs, steps, rates, lens, sems
):
    count = out_ref.shape[0]
    heads_dev = dt_ref.shape[1] // count
    width = x_ref.shape[1] // count
    copies = [
        pltpu.make_async_copy(src, dst, sems.at[i])
        for i, (src, dst) in enumerate(
            ((x_ref, xs), (b_ref, bs), (dt_ref, steps), (rate_ref, rates), (len_ref, lens))
        )
    ]
    for copy in copies:
        copy.start()
    for copy in copies:
        copy.wait()
    raw = steps[...].astype(f32)
    raw = jnp.concatenate([raw, jnp.zeros((raw.shape[0], STATE - raw.shape[1]), f32)], axis=1)
    for d in range(count):
        out_ref[d, :, 0:width] = xs[:, d * width : (d + 1) * width]
        out_ref[d, :, width : width + STATE] = bs[:, d * STATE : (d + 1) * STATE]
        mine = raw if d == 0 else pltpu.roll(raw, STATE - d * heads_dev, 1)
        out_ref[d, :, width + STATE : width + 2 * STATE] = mine.astype(bf16)
    meta_ref[...] = jnp.zeros_like(meta_ref)
    meta_ref[0:1, 0 : rates.shape[1]] = rates[...]
    meta_ref[1:2, 0:1] = lens[:, 0:1].astype(f32)
    meta_ref[2:3, 0:1] = (lens[:, 0:1] + lens[:, 1:2]).astype(f32)


def pack_gates(me_ref, after_ref, z_ref, c_ref, keep_ref, give_ref):
    del after_ref
    chips = keep_ref.shape[0]
    width = z_ref.shape[1] // (2 * chips)
    for side, ref in enumerate((keep_ref, give_ref)):
        for k in range(chips):
            peer = me_ref[0] ^ (2 * k + side)
            z_start = pl.multiple_of(peer * width, STATE)
            c_start = pl.multiple_of(peer * STATE, STATE)
            ref[k, :, 0:width] = z_ref[:, pl.ds(z_start, width)]
            ref[k, :, width : width + STATE] = c_ref[:, pl.ds(c_start, STATE)]


def pair_up(keep_ref, got_ref, *out_refs):
    for k, ref in enumerate(out_refs):
        ref[0] = keep_ref[k]
        ref[1] = got_ref[k]


def exchange(keep, give, n_head):
    chips = n_head // 2
    shape = jax.ShapeDtypeStruct((2,) + keep.shape[1:], bf16)
    got = lax.ppermute(give, "head", [(i, i ^ 1) for i in range(n_head)])
    pairs = pl.pallas_call(
        pair_up,
        out_shape=[shape] * chips,
        in_specs=[VMEM] * 2,
        out_specs=[VMEM] * chips,
        compiler_params=params(),
        cost_estimate=cost(0, 800_000),
    )(keep, got)
    return [pairs[0]] + [
        lax.ppermute(pairs[k], "head", [(i, i ^ (2 * k)) for i in range(n_head)])
        for k in range(1, chips)
    ]


def fetch(me, pair_refs, rows_ref, sems):
    rows = pair_refs[0].shape[1]
    copies = []
    for k, ref in enumerate(pair_refs):
        for side in range(2):
            start = pl.multiple_of((me ^ (2 * k + side)) * rows, rows)
            copies.append(
                pltpu.make_async_copy(
                    ref.at[side], rows_ref.at[pl.ds(start, rows), :], sems.at[2 * k + side]
                )
            )
    for copy in copies:
        copy.start()
    return copies


def pack_cache(cache_ref, out_ref):
    for s in range(SLOTS):
        out_ref[:, s * STATE : (s + 1) * STATE] = cache_ref[s].astype(bf16)


def segment_of(position, ends):
    return (position >= ends[0]).astype(jnp.int32) + (position >= ends[1]).astype(jnp.int32)


def segment_ends(meta_ref):
    return meta_ref[1:2, 0:1].astype(jnp.int32), meta_ref[2:3, 0:1].astype(jnp.int32)


def spread_heads(heads, width):
    row = lax.broadcasted_iota(jnp.int32, (heads, width), 0)
    column = lax.broadcasted_iota(jnp.int32, (heads, width), 1)
    return (row == column // (width // heads)).astype(bf16)


def local_state(meta_ref, tok_ref, send_ref, out_ref, made, sems):
    del send_ref
    length = tok_ref.shape[0]
    width = out_ref.shape[0]
    heads = width // HEAD_DIM
    ends = segment_ends(meta_ref)
    step_size = jax.nn.softplus(tok_ref[:, width + STATE : width + STATE + heads].astype(f32))
    log_decay = -step_size * meta_ref[0:1, 0:heads]
    row = lax.broadcasted_iota(jnp.int32, (length, length), 0)
    column = lax.broadcasted_iota(jnp.int32, (length, length), 1)
    later = (segment_of(row, ends) == segment_of(column, ends)) & (column > row)
    after = exact_left(later.astype(f32).astype(bf16), log_decay)
    weight = exact_right(jnp.exp(after) * step_size, spread_heads(heads, width), 2)
    scaled = (weight * tok_ref[:, 0:width].astype(f32)).astype(bf16)
    token = lax.broadcasted_iota(jnp.int32, (length, STATE), 0)
    lane = lax.broadcasted_iota(jnp.int32, (length, STATE), 1)
    seg_index = segment_of(token, ends)
    b_half = tok_ref[:, width : width + STATE].astype(f32)
    b_parts = jnp.concatenate(
        [jnp.where(seg_index == j, b_half, 0.0).astype(bf16) for j in range(REQS)], axis=1
    )
    made[:, 0 : REQS * STATE] = dot_tn(scaled, b_parts).astype(bf16)
    start, middle = SLOTS * STATE, (SLOTS + REQS) * STATE
    early = pltpu.make_async_copy(
        made.at[:, 0 : REQS * STATE], out_ref.at[:, start:middle], sems.at[0]
    )
    early.start()
    member = (seg_index == lane % REQS).astype(f32).astype(bf16)
    total = None
    for piece in split(log_decay, 3):
        term = dot_tn(piece, member)
        total = term if total is None else total + term
    kept = jnp.exp(total)
    high = kept.astype(bf16).astype(f32)
    lane_h = lax.broadcasted_iota(jnp.int32, (heads, STATE), 1)
    parts = jnp.where(lane_h < REQS, high, jnp.where(lane_h < 2 * REQS, kept - high, 0.0))
    row_w = lax.broadcasted_iota(jnp.int32, (width, heads), 0)
    col_w = lax.broadcasted_iota(jnp.int32, (width, heads), 1)
    owner = (row_w // HEAD_DIM == col_w).astype(f32).astype(bf16)
    spread = dot(owner, parts.astype(bf16))
    row_s = lax.broadcasted_iota(jnp.int32, (width, STATE), 0)
    lane_s = lax.broadcasted_iota(jnp.int32, (width, STATE), 1)
    chosen = jnp.where(lane_s == row_s % ROWS, spread, 0.0).astype(bf16)
    made[:, REQS * STATE :] = dot(chosen, jnp.ones((STATE, STATE), bf16)).astype(bf16)
    last = pltpu.make_async_copy(made.at[:, REQS * STATE :], out_ref.at[:, middle:], sems.at[1])
    last.start()
    early.wait()
    last.wait()


def combine(hit_ref, place_ref, recv_ref, *refs):
    out_ref, held, picked, made, sems = refs[-5:]
    first, half = SLOTS * STATE, REQS * STATE
    for s in range(recv_ref.shape[0]):
        block = recv_ref[s, :, 0:first].astype(f32)
        for k in range(SLOTS):
            held[s * SLOTS + k] = block[:, k * STATE : (k + 1) * STATE]
    for s in range(recv_ref.shape[0]):
        for j in range(REQS):
            picked[s, :, j * STATE : (j + 1) * STATE] = held[hit_ref[s * REQS + j]].astype(bf16)
    early = pltpu.make_async_copy(picked, out_ref.at[:, :, 0:half], sems.at[0])
    early.start()
    for s in range(recv_ref.shape[0]):
        block = recv_ref[s, :, first:].astype(f32)
        prefix = picked[s].astype(f32)
        kept = block[:, half:]
        for j in range(REQS):
            columns = slice(j * STATE, (j + 1) * STATE)
            factor = kept[j : j + 1, :] + kept[REQS + j : REQS + j + 1, :]
            new = factor * prefix[:, columns] + block[:, columns]
            place = place_ref[s * REQS + j]
            start = pl.multiple_of((place & 3) * STATE, STATE)
            made[place >> 2, :, pl.ds(start, STATE)] = new.astype(bf16)
    last = pltpu.make_async_copy(made, out_ref.at[:, :, half:], sems.at[1])
    last.start()
    early.wait()
    last.wait()


def token_inner(me_ref, meta_ref, skip_ref, tok_ref, *refs):
    pair_refs, (base_ref, factor_ref, read_ref, gates, sems) = refs[:-5], refs[-5:]
    length = tok_ref.shape[0]
    heads = skip_ref.shape[1]
    width = heads * HEAD_DIM
    copies = fetch(me_ref[0], pair_refs, gates, sems)
    ends = segment_ends(meta_ref)
    step_size = jax.nn.softplus(tok_ref[:, width + STATE : width + STATE + heads].astype(f32))
    log_decay = -step_size * meta_ref[0:1, 0:heads]
    row = lax.broadcasted_iota(jnp.int32, (length, length), 0)
    column = lax.broadcasted_iota(jnp.int32, (length, length), 1)
    upto = (segment_of(row, ends) == segment_of(column, ends)) & (column <= row)
    running = exact_left(upto.astype(f32).astype(bf16), log_decay)
    spread = spread_heads(heads, width)
    decay = exact_right(jnp.exp(running), spread)
    undo = exact_right(jnp.exp(-running) * step_size, spread, 2)
    values = tok_ref[:, 0:width].astype(f32)
    b_half = tok_ref[:, width : width + STATE]
    for copy in copies:
        copy.wait()
    c_half = gates[:, width : width + STATE]
    c_wide = c_half.astype(f32)
    scores = jnp.where(upto, dot_nt(c_half, b_half), 0.0).astype(bf16)
    token = lax.broadcasted_iota(jnp.int32, (length, STATE), 0)
    seg_index = segment_of(token, ends)
    for j in range(REQS):
        read_ref[:, j * STATE : (j + 1) * STATE] = jnp.where(seg_index == j, c_wide, 0.0).astype(
            bf16
        )
    inner = dot(scores, (undo * values).astype(bf16))
    gate_in = gates[:, 0:width].astype(f32)
    gate = gate_in / (1.0 + jnp.exp(-gate_in))
    base_ref[...] = gate * (decay * inner + exact_right(skip_ref[...], spread) * values)
    factor_ref[...] = gate * decay


def finish(
    missing_ref, cache_ref, gain_ref, base_ref, factor_ref, read_ref, recv_ref,
    rows_ref, states_ref, rows, states, sems,
):
    missing = missing_ref[0]
    first = REQS * STATE
    copies = []
    for s in range(SLOTS):

        @pl.when(missing == s)
        def _():
            states[s] = cache_ref[s]

        if s < REQS:

            @pl.when(missing > s)
            def _():
                states[s] = recv_ref[:, first + s * STATE : first + (s + 1) * STATE].astype(f32)

        if s > 0:

            @pl.when(missing < s)
            def _():
                states[s] = recv_ref[:, first + (s - 1) * STATE : first + s * STATE].astype(f32)

        copies.append(pltpu.make_async_copy(states.at[s], states_ref.at[s], sems.at[s]))
        copies[-1].start()
    carried = dot_nt(read_ref[...], recv_ref[:, 0:first])
    gated = base_ref[...] + factor_ref[...] * carried
    square_mean = jnp.mean(gated * gated, axis=1, keepdims=True)
    rows[...] = (gated * lax.rsqrt(square_mean + 1e-05) * gain_ref[...]).astype(bf16)
    copies.append(pltpu.make_async_copy(rows, rows_ref, sems.at[SLOTS]))
    copies[-1].start()
    for copy in copies:
        copy.wait()


def gated_norm(values, gate_in, norm_weight):
    shaped = values.shape
    gated = values * jax.nn.silu(gate_in.astype(jnp.float32).reshape(shaped))
    square_mean = jnp.mean(gated * gated, axis=(2, 3), keepdims=True)
    normed = gated * lax.rsqrt(square_mean + 1e-05) * norm_weight.reshape(shaped[1:])
    return normed.reshape(shaped[0], -1).astype(jnp.bfloat16)


def decode_block(
    inputs, gate_in, b_proj, c_proj, step_raw, states, head_rates, skip_gain, norm_weight
):
    row_count = inputs.shape[0]
    head_count = step_raw.shape[1]
    groups = b_proj.shape[1] // STATE
    per_group = head_count // groups
    step_size = jax.nn.softplus(step_raw.astype(jnp.float32))
    factor = jnp.exp(-step_size * head_rates[None, :]).reshape(row_count, groups, per_group, 1, 1)
    values = inputs.astype(jnp.float32).reshape(row_count, groups, per_group, HEAD_DIM)
    b_group = b_proj.astype(jnp.float32).reshape(row_count, groups, STATE)
    c_group = c_proj.astype(jnp.float32).reshape(row_count, groups, STATE)
    written = (step_size.reshape(row_count, groups, per_group, 1) * values)[..., None] * b_group[
        :, :, None, None, :
    ]
    updated = factor * states.reshape(row_count, groups, per_group, HEAD_DIM, STATE) + written
    outputs = (
        jnp.einsum("rgkpn,rgn->rgkp", updated, c_group, precision=highest)
        + skip_gain.reshape(groups, per_group, 1) * values
    )
    return (
        gated_norm(outputs, gate_in, norm_weight),
        updated.reshape(row_count, head_count, HEAD_DIM, STATE),
    )


def local(
    pre_x,
    pre_z,
    pre_b,
    pre_c,
    pre_dt,
    suffix_lengths,
    prefix_hits,
    snapshot_slots,
    cache_states,
    dec_x,
    dec_z,
    dec_b,
    dec_c,
    dec_dt,
    dec_states,
    decay_rate,
    d_skip,
    norm_weight,
):
    n_head = lax.axis_size("head")
    n_serve = lax.axis_size("serve")
    rows = pre_x.shape[0]
    heads = cache_states.shape[1]
    width = heads * HEAD_DIM
    length = rows * n_head
    tiles = SLOTS + REQS + 1
    shape = jax.ShapeDtypeStruct

    def swap(value, axis):
        return lax.all_to_all(value, axis, split_axis=0, concat_axis=0, tiled=True)

    chips = n_head // 2
    with jax.named_scope("tokens"):
        first, meta = pl.pallas_call(
            pack_first,
            out_shape=(
                shape((n_head, rows, width + 2 * STATE), bf16),
                shape((8, STATE), f32),
            ),
            in_specs=[HBM] * 5,
            out_specs=(VMEM, VMEM),
            scratch_shapes=[
                pltpu.VMEM(pre_x.shape, bf16),
                pltpu.VMEM(pre_b.shape, bf16),
                pltpu.VMEM(pre_dt.shape, bf16),
                pltpu.VMEM((1, heads), f32),
                pltpu.VMEM(suffix_lengths.shape, jnp.int32),
                pltpu.SemaphoreType.DMA((5,)),
            ],
            compiler_params=params(56),
            cost_estimate=cost(0, 800_000),
        )(pre_x, pre_b, pre_dt, decay_rate.reshape(1, heads), suffix_lengths)
        tokens = swap(first, "head").reshape(length, width + 2 * STATE)
    with jax.named_scope("cache"):
        cache_rows = cache_states.reshape(SLOTS, width, STATE)
        send = pl.pallas_call(
            pack_cache,
            out_shape=shape((width, tiles * STATE), bf16),
            grid=(1,),
            in_specs=[VMEM],
            out_specs=pl.BlockSpec((width, SLOTS * STATE), lambda i: (0, 0)),
            compiler_params=params(),
            cost_estimate=cost(0, 1_600_000),
        )(cache_rows)
    with jax.named_scope("orders"):
        rank = jnp.sum(
            (snapshot_slots[None, :] < snapshot_slots[:, None]).astype(jnp.int32), axis=1
        )
        place = (rank // REQS) * 4 + rank % REQS
        serve_me = lax.axis_index("serve")
        missing = (
            sum(range(SLOTS))
            - jnp.sum(jnp.where(snapshot_slots // SLOTS == serve_me, snapshot_slots % SLOTS, 0))
        ).reshape(1)
        head_me = lax.axis_index("head").astype(jnp.int32).reshape(1)
    with jax.named_scope("local"):
        send = pl.pallas_call(
            local_state,
            out_shape=shape((width, tiles * STATE), bf16),
            in_specs=[VMEM, VMEM, HBM],
            out_specs=HBM,
            scratch_shapes=[
                pltpu.VMEM((width, (REQS + 1) * STATE), bf16),
                pltpu.SemaphoreType.DMA((2,)),
            ],
            input_output_aliases={2: 0},
            compiler_params=params(),
            cost_estimate=cost(300_000_000, 800_000),
        )(meta, tokens, send)
        pieces = swap(send.reshape(n_serve, ROWS, tiles * STATE), "serve")
    with jax.named_scope("gates"):
        keep, give = pl.pallas_call(
            pack_gates,
            out_shape=[shape((chips, rows, width + STATE), bf16)] * 2,
            in_specs=[SMEM, ANY] + [VMEM] * 2,
            out_specs=[VMEM] * 2,
            compiler_params=params(),
            cost_estimate=cost(0, 650_000),
        )(head_me, send, pre_z, pre_c)
        gates = exchange(keep, give, n_head)
    with jax.named_scope("combine"):
        answer = pl.pallas_call(
            combine,
            out_shape=shape((n_serve, ROWS, 2 * REQS * STATE), bf16),
            in_specs=[SMEM, SMEM, VMEM] + [ANY] * (chips - 1),
            out_specs=HBM,
            scratch_shapes=[
                pltpu.VMEM((n_serve * SLOTS, ROWS, STATE), f32),
                pltpu.VMEM((n_serve, ROWS, REQS * STATE), bf16),
                pltpu.VMEM((n_serve, ROWS, REQS * STATE), bf16),
                pltpu.SemaphoreType.DMA((2,)),
            ],
            compiler_params=params(),
            cost_estimate=cost(0, 4_000_000),
        )(prefix_hits, place, pieces, *gates[1:])
        got = swap(answer, "serve").reshape(width, 2 * REQS * STATE)
    with jax.named_scope("inner"):
        base, factor, read = pl.pallas_call(
            token_inner,
            out_shape=(
                shape((length, width), f32),
                shape((length, width), f32),
                shape((length, REQS * STATE), bf16),
            ),
            in_specs=[SMEM] + [VMEM] * 3 + [ANY] * chips,
            out_specs=[VMEM] * 3,
            scratch_shapes=[
                pltpu.VMEM((length, width + STATE), bf16),
                pltpu.SemaphoreType.DMA((n_head,)),
            ],
            compiler_params=params(),
            cost_estimate=cost(400_000_000, 1_500_000),
        )(head_me, meta, d_skip.reshape(1, heads), tokens, *gates)
    dec_out, dec_new = decode_block(
        dec_x, dec_z, dec_b, dec_c, dec_dt, dec_states, decay_rate, d_skip, norm_weight
    )
    with jax.named_scope("outputs"):
        pre_out, cache_out = pl.pallas_call(
            finish,
            out_shape=(shape((length, width), bf16), shape((SLOTS, width, STATE), f32)),
            in_specs=[SMEM] + [VMEM] * 6,
            out_specs=(HBM, HBM),
            scratch_shapes=[
                pltpu.VMEM((length, width), bf16),
                pltpu.VMEM((SLOTS, width, STATE), f32),
                pltpu.SemaphoreType.DMA((SLOTS + 1,)),
            ],
            compiler_params=params(),
            cost_estimate=cost(200_000_000, 4_000_000),
        )(missing, cache_rows, norm_weight.reshape(1, width), base, factor, read, got)
        cache_out = cache_out.reshape(cache_states.shape)
    return (pre_out, cache_out, dec_out, dec_new)


def solution(mesh):
    return jax.shard_map(
        local,
        mesh=mesh,
        in_specs=(
            P(("serve", "head"), None),
            P(("serve", "head"), None),
            P(("serve", "head"), None),
            P(("serve", "head"), None),
            P(("serve", "head"), None),
            P("serve", None),
            P(),
            P(),
            P("serve", "head", None, None),
            P("serve", "head"),
            P("serve", "head"),
            P("serve", "head"),
            P("serve", "head"),
            P("serve", "head"),
            P("serve", "head", None, None),
            P("head"),
            P("head"),
            P("head"),
        ),
        out_specs=(
            P("serve", "head"),
            P("serve", "head", None, None),
            P("serve", "head"),
            P("serve", "head", None, None),
        ),
        check_vma=False,
    )
```
